256 devices in a mesh: blk: 16 (over y_hi, x, core), space: 16 (over y_lo, z).
Axes of the slice: x: 4, y: 4 (y_hi: 2, y_lo: 2; y = y_hi * 2 + y_lo), z: 8, core: 2. Of those that a mesh axis runs over, the one named last changes fastest.
Arguments:
- electrons: bfloat16 [16, 8, 2, 64, 4096], P('blk', None, None, 'space'), may hold values from -4 to 4
- holes: bfloat16 [16, 8, 2, 64, 4096], P('blk', None, None, 'space'), may hold values from -4 to 4
- pair_order: int32 [16, 2], P('blk'), may hold values from 0 to 1, each once within a row
Outputs:
- potential: float32 [16, 2, 64, 64, 128], P('blk', None, 'space')
- coulomb: float32 [16, 2, 2, 2], P('blk')
The draws below stay inside these ranges and needn't reach their ends.
Inputs may be any that keep to these rules, and one draw needn't show every extreme that they name: `pair_order`: each row lists every candidate once.
All inputs are finite; a program needn't handle non-finite values.
Results may differ from the reference program's by a relative error of at most 0.0003.
Values may be sent and summed in bfloat16 or wider, within the bound.
No kernel may reach another device: no remote copies, remote signals or barrier semaphores. Data moves between devices by JAX's collectives and lax.ppermute only.
A program may use at most 64 MiB of HBM per device.

```python
import math
import jax
import jax.numpy as jnp
from jax import lax

BANDS = 8
NX = 64
NY = 64
NZ = 64
EG = 1
HG = 1
GROUPS = 16
E = 16
H = 16
P_SIZE = 2


def dot_envelopes(key, amount):
    keys = jax.random.split(key, 5)
    centre_x = jax.random.uniform(keys[0], (amount,), jnp.float32, 0.3, 0.7)
    centre_y = jax.random.uniform(keys[1], (amount,), jnp.float32, 0.3, 0.7)
    upper_dot = jax.random.randint(keys[2], (amount,), 0, 2).astype(jnp.float32)
    centre_z = 0.35 + 0.3 * upper_dot + jax.random.uniform(keys[3], (amount,), jnp.float32, -0.05, 0.05)
    spread = jax.random.uniform(keys[4], (amount,), jnp.float32, 0.12, 0.25)
    grid_x = (jnp.arange(NX, dtype=jnp.float32) + 0.5) / NX
    grid_y = (jnp.arange(NY, dtype=jnp.float32) + 0.5) / NY
    grid_z = (jnp.arange(NZ, dtype=jnp.float32) + 0.5) / NZ
    distance = (grid_x[None, :, None, None] - centre_x[:, None, None, None]) ** 2
    distance = distance + (grid_y[None, None, :, None] - centre_y[:, None, None, None]) ** 2
    distance = distance + (grid_z[None, None, None, :] - centre_z[:, None, None, None]) ** 2
    envelope = jnp.exp(-distance / (2.0 * spread[:, None, None, None] ** 2))
    return envelope.reshape(amount, NX, NY * NZ)


def draw_states(key, amount, salt):
    own_key = jax.random.fold_in(key, salt)
    keys = jax.random.split(own_key, 3)
    envelope = dot_envelopes(keys[0], amount)
    amplitude = jax.random.normal(keys[1], (amount, BANDS, 2, 1, 1), jnp.float32)
    rough = jax.random.normal(keys[2], (amount, BANDS, 2, NX, NY * NZ), jnp.float32)
    scaling = jnp.ones((amount, 1, 1, 1, 1), jnp.float32)
    modulated = (0.2 + envelope[:, None, None]) * amplitude
    spread = jnp.sqrt(modulated * modulated + 0.36)
    states = 0.25 * scaling * rough * spread
    return jnp.clip(states, -4.0, 4.0).astype(jnp.bfloat16)


def draw_electrons(key, part):
    return draw_states(key, E, 11)


def draw_holes(key, part):
    return draw_states(key, H, 12)


def setup_inputs(seed: int = 0) -> dict:
    arg_keys = jax.random.split(jax.random.key(seed), 4)
    return {
        "electrons": draw_electrons(jax.random.fold_in(arg_keys[3], 71), 0),
        "holes": draw_holes(jax.random.fold_in(arg_keys[3], 71), 0),
        "pair_order": jax.vmap(lambda own: jax.random.permutation(own, P_SIZE))(jax.random.split(arg_keys[2], GROUPS)).reshape((GROUPS, P_SIZE)).astype(jnp.int32),
    }


SCREENING = 0.01


def lattice_term(indices, points):
    return 2.0 - 2.0 * jnp.cos((2.0 * math.pi / points) * (indices % points).astype(jnp.float32))


def reference(electrons, holes, pair_order):
    index_x = jnp.arange(NX, dtype=jnp.int32)
    index_y = jnp.arange(NY, dtype=jnp.int32)
    index_z = jnp.arange(NZ, dtype=jnp.int32)
    term_x = lattice_term(index_x, NX)
    term_y = lattice_term(index_y, NY)
    term_z = lattice_term(index_z, NZ)
    green = 1.0 / (term_x[:, None, None] + term_y[None, :, None] + term_z[None, None, :] + SCREENING)
    anchor = (index_x[:, None, None] == 0) & (index_y[None, :, None] == 0) & (index_z[None, None, :] == 0)
    green = jnp.where(anchor, jnp.zeros_like(green), green)
    cells = NX * NY * NZ

    def banded(first_set, second_set):
        return jnp.einsum("ebxc,hbxc->hexc", first_set, second_set, precision=lax.Precision.HIGHEST)

    def one_group(group):
        group = group.astype(jnp.int32)
        prior = jnp.mod(group - 1 + GROUPS, GROUPS).astype(jnp.int32)
        elec = lax.dynamic_slice_in_dim(electrons, (group * EG).astype(jnp.int32), EG, 0).astype(jnp.float32)
        hole_own = lax.dynamic_slice_in_dim(holes, (group * HG).astype(jnp.int32), HG, 0)
        hole_far = lax.dynamic_slice_in_dim(holes, (prior * HG).astype(jnp.int32), HG, 0)
        hole_set = jnp.concatenate([hole_own, hole_far], axis=0).astype(jnp.float32)
        real_part = banded(elec[:, :, 0], hole_set[:, :, 0]) + banded(elec[:, :, 1], hole_set[:, :, 1])
        imag_part = banded(elec[:, :, 0], hole_set[:, :, 1]) - banded(elec[:, :, 1], hole_set[:, :, 0])
        target_shape = (P_SIZE, NX, NY, NZ)
        densities = lax.complex(real_part.reshape(target_shape), imag_part.reshape(target_shape))
        spectra = jnp.fft.fftn(densities, axes=(1, 2, 3))
        field = jnp.fft.ifftn(spectra * green[None], axes=(1, 2, 3))
        pair_rank = pair_order[group]
        field = jnp.take(field, pair_rank, axis=0)
        densities = jnp.take(densities, pair_rank, axis=0)
        flat_field = field.reshape(P_SIZE, -1)
        flat_dens = jnp.conj(densities.reshape(P_SIZE, -1))
        product = jnp.einsum("pn,qn->pq", flat_field, flat_dens, precision=lax.Precision.HIGHEST) / cells
        potential = jnp.concatenate([jnp.real(field), jnp.imag(field)], axis=-1)
        coulomb = jnp.stack([jnp.real(product), jnp.imag(product)])
        return potential, coulomb

    potential, coulomb = lax.map(one_group, jnp.arange(GROUPS, dtype=jnp.int32))
    return potential, coulomb
```

```python
import math

import jax
import jax.numpy as jnp
import numpy as np
from jax import lax
from jax.experimental import pallas as pl
from jax.experimental.pallas import tpu as pltpu
from jax.sharding import PartitionSpec as P

NX = 64
NY = 64
NZ = 64
CELLS = NX * NY * NZ
SCREENING = 0.01
PARTS = 16
PLANES = NX // PARTS
HALF = NY // 2
ROWS = HALF * PLANES
LANES = 128


def turn(angles, sign):
    cosines, sines = np.cos(angles), sign * np.sin(angles)
    return np.array([[cosines, -sines], [sines, cosines]])


def tables():
    half, full = np.arange(HALF), np.arange(NY)
    planes, two = np.arange(PLANES), np.arange(2)
    eye_x, eye_2 = np.eye(PLANES), np.eye(2)
    rows = turn(2 * math.pi * (np.outer(half, half) % HALF) / HALF, -1)
    first = np.einsum("dckn,yx->dkycnx", rows, eye_x).reshape(2 * ROWS, 2 * ROWS)
    angles = 2 * math.pi / NY * half[:, None, None, None] * two[None, None, :, None]
    angles = np.broadcast_to(angles, (HALF, PLANES, 2, NZ)).reshape(ROWS, LANES)
    twiddle = np.stack([np.cos(angles), np.sin(angles)])
    depth = turn(2 * math.pi * (np.outer(full, full) % NZ) / NZ, -1)
    signs = np.array([[1.0, 1.0], [1.0, -1.0]])
    second = np.einsum("dckz,hb->cbzdhk", depth, signs).reshape(2 * LANES, 2 * LANES)
    across = turn(2 * math.pi * (np.outer(full, full) % NX) / NX, -1)
    across = across.reshape(2, 2, NX, PARTS, PLANES)
    third = np.einsum("dcksx,lm->dlkscmx", across, eye_2).reshape(256, 256)
    fourth = third.T
    columns = turn(2 * math.pi * (np.outer(full, half) % NY) / NY, 1)
    columns = columns.reshape(2, 2, NY, PARTS, 2)
    fifth = np.einsum("dcysl,vx->dvysclx", columns, eye_x).reshape(512, 256)
    back = turn(2 * math.pi * (np.outer(full, full) % NZ) / NZ, 1)
    sixth = np.einsum("dczk,h->chkdz", back, np.ones(2)).reshape(256, 128)
    parity = np.ones((NY, 2, NZ))
    parity[1::2, 1] = -1.0
    parity = np.tile(parity.reshape(NY, LANES), (PLANES, 1))
    term = 2.0 - 2.0 * np.cos(2 * math.pi * full / 64)
    base = term[None, :, None, None] + term[None, None, None, :] + SCREENING
    base = np.broadcast_to(base, (2, NX, 2, NZ)).reshape(128, LANES)
    term_y = term.reshape(2, HALF).T
    term_y = np.repeat(term_y, NZ, axis=1)
    names = ("first", "twiddle", "second", "third", "fourth", "fifth", "sixth", "parity", "base", "term_y")
    values = (first, twiddle, second, third, fourth, fifth, sixth, parity, base, term_y)
    return {n: np.ascontiguousarray(v, dtype=np.float32) for n, v in zip(names, values)}


def dot(a, b):
    return jnp.dot(a, b, precision=lax.Precision.HIGHEST, preferred_element_type=jnp.float32)


def density_spectra(electrons, holes, first, twiddle, second):
    real = jnp.zeros((ROWS, LANES), jnp.float32)
    imag = jnp.zeros((ROWS, LANES), jnp.float32)
    for band in range(electrons.shape[0]):
        e_re = electrons[band, 0].astype(jnp.float32)
        e_im = electrons[band, 1].astype(jnp.float32)
        h_re = holes[band, 0].astype(jnp.float32)
        h_im = holes[band, 1].astype(jnp.float32)
        real += e_re * h_re + e_im * h_im
        imag += e_re * h_im - e_im * h_re
    mixed = dot(first[...], jnp.concatenate([real, imag], axis=0))
    u_re, u_im = mixed[:ROWS], mixed[ROWS:]
    t_re = u_re * twiddle[0] + u_im * twiddle[1]
    t_im = u_im * twiddle[0] - u_re * twiddle[1]
    return dot(jnp.concatenate([t_re, t_im], axis=1), second[...])


def own_kernel(rank, electrons, holes, first, twiddle, second, base, term_y, out, green):
    spectra = density_spectra(electrons, holes, first, twiddle, second)
    for c in range(2):
        out[:, c] = spectra[:, c * LANES : (c + 1) * LANES].reshape(PARTS, 8, LANES)
    me = rank[0]
    row = lax.broadcasted_iota(jnp.int32, (NX, LANES), 0)
    lane = lax.broadcasted_iota(jnp.int32, (NX, LANES), 1)
    for kl in range(2):
        block = base[kl * NX : (kl + 1) * NX] + term_y[pl.ds(2 * me + kl, 1), :]
        value = (1.0 / CELLS) / block
        if kl == 0:
            value = jnp.where((row == 0) & (lane == 0) & (me == 0), 0.0, value)
        green[kl * NX : (kl + 1) * NX] = value


def far_kernel(order, electrons, holes, own, first, twiddle, second, out):
    spectra = density_spectra(electrons, holes, first, twiddle, second)
    straight = order[0, 0] == 0
    for c in range(2):
        far = spectra[:, c * LANES : (c + 1) * LANES].reshape(PARTS, 8, LANES)
        near = own[:, c]
        out[:, 0, c] = jnp.where(straight, near, far)
        out[:, 1, c] = jnp.where(straight, far, near)


def screen_kernel(block, green, third, fourth, out):
    columns = [block[:, p].reshape(256, LANES) for p in range(2)]
    spectra = dot(third[...], jnp.concatenate(columns, axis=1))
    weight = green[...]
    weight = jnp.concatenate([weight, weight], axis=0)
    s0, s1 = spectra[:, :LANES], spectra[:, LANES:]
    w0, w1 = s0 * weight, s1 * weight
    back = dot(fourth[...], jnp.concatenate([w0, w1], axis=1))
    for p in range(2):
        out[:, p * 16 : (p + 1) * 16] = back[:, p * LANES : (p + 1) * LANES].reshape(PARTS, 16, LANES)
    terms = [
        jnp.sum(w0 * s0, axis=0, keepdims=True),
        jnp.sum(w1 * s1, axis=0, keepdims=True),
        jnp.sum(w0 * s1, axis=0, keepdims=True),
        jnp.sum(w0[128:] * s1[:128] - w0[:128] * s1[128:], axis=0, keepdims=True),
    ]
    part = jnp.concatenate(terms + [jnp.zeros((4, LANES), jnp.float32)], axis=0)
    out[:, 32:40] = jnp.broadcast_to(part[None], (PARTS, 8, LANES))


def field_kernel(block, fifth, sixth, parity, potential, coulomb):
    columns = [block[:, p * 16 : (p + 1) * 16].reshape(256, LANES) for p in range(2)]
    mixed = dot(fifth[...], jnp.concatenate(columns, axis=1))
    signs = parity[...]
    for p in range(2):
        own = mixed[:, p * LANES : (p + 1) * LANES]
        lanes = jnp.concatenate([own[:256] * signs, own[256:] * signs], axis=1)
        potential[p] = dot(lanes, sixth[...]).reshape(PLANES, NY, LANES)
    sums = jnp.sum(jnp.sum(block[:, 32:40], axis=0), axis=1, keepdims=True) * (1.0 / CELLS)
    c00, c11, re, im = (sums[k : k + 1] for k in range(4))
    row = lax.broadcasted_iota(jnp.int32, (2, 2), 0)
    col = lax.broadcasted_iota(jnp.int32, (2, 2), 1)
    coulomb[0] = jnp.where(row == col, jnp.where(row == 0, c00, c11), re)
    coulomb[1] = jnp.where(row == col, 0.0, jnp.where(row == 0, im, -im))


def full(memory_space=pltpu.VMEM):
    return pl.BlockSpec(memory_space=memory_space)


def call(kernel, name, out_shape, *operands, scalars=0):
    specs = [full(pltpu.SMEM)] * scalars + [full()] * (len(operands) - scalars)
    several = isinstance(out_shape, (list, tuple))
    return pl.pallas_call(
        kernel,
        out_shape=out_shape,
        in_specs=specs,
        out_specs=[full()] * len(out_shape) if several else full(),
        compiler_params=pltpu.CompilerParams(vmem_limit_bytes=32 * 1024 * 1024),
        name=name,
    )(*operands)


def shape(*dims):
    return jax.ShapeDtypeStruct(dims, jnp.float32)


def tiled_states(states):
    bands = states.shape[1]
    parts = states.reshape(bands, 2, PLANES, HALF, LANES)
    return parts.transpose(0, 1, 3, 2, 4).reshape(bands, 2, ROWS, LANES)


def shards(electrons, holes, pair_order):
    t = {name: jnp.asarray(value) for name, value in tables().items()}
    groups = lax.axis_size("blk")
    rank = lax.axis_index("space").astype(jnp.int32).reshape(1)
    previous = lax.ppermute(holes, "blk", [((i - 1) % groups, i) for i in range(groups)])
    e = tiled_states(electrons)
    own, green = call(
        own_kernel, "own_pair", [shape(PARTS, 2, 8, LANES), shape(128, LANES)],
        rank, e, tiled_states(holes), t["first"], t["twiddle"], t["second"], t["base"], t["term_y"], scalars=1,
    )
    sent = call(
        far_kernel, "far_pair", shape(PARTS, 2, 2, 8, LANES),
        pair_order, e, tiled_states(previous), own, t["first"], t["twiddle"], t["second"], scalars=1,
    )
    columns = lax.all_to_all(sent, "space", split_axis=0, concat_axis=0, tiled=True)
    screened = call(
        screen_kernel, "screen", shape(PARTS, 40, LANES), columns, green, t["third"], t["fourth"]
    )
    fields = lax.all_to_all(screened, "space", split_axis=0, concat_axis=0, tiled=True)
    potential, coulomb = call(
        field_kernel, "field", [shape(2, PLANES, NY, LANES), shape(2, 2, 2)],
        fields, t["fifth"], t["sixth"], t["parity"],
    )
    return (potential[None], coulomb[None])


def solution(mesh):
    in_specs = (
        P("blk", None, None, "space", None),
        P("blk", None, None, "space", None),
        P("blk", None),
    )
    out_specs = (P("blk", None, "space", None, None), P("blk", None, None, None))
    return jax.shard_map(shards, mesh=mesh, in_specs=in_specs, out_specs=out_specs, check_vma=False)
```

```python
import math

import jax
import jax.numpy as jnp
import ml_dtypes
import numpy as np
from jax import lax
from jax.experimental import pallas as pl
from jax.experimental.pallas import tpu as pltpu
from jax.sharding import PartitionSpec as P

NX = 64
NY = 64
NZ = 64
CELLS = NX * NY * NZ
SCREENING = 0.01
PARTS = 16
PLANES = NX // PARTS
HALF = NY // 2
ROWS = HALF * PLANES
LANES = 128


def turn(angles, sign):
    cosines, sines = np.cos(angles), sign * np.sin(angles)
    return np.array([[cosines, -sines], [sines, cosines]])


def tables():
    half, full = np.arange(HALF), np.arange(NY)
    two = np.arange(2)
    eye_x = np.eye(PLANES)
    order = np.array([2 * d + kl for kl in range(2) for d in range(PARTS)])
    rows = turn(2 * math.pi * (np.outer(order, half) % HALF) / HALF, -1)
    first = np.einsum("dckn,yx->dykcnx", rows, eye_x).reshape(2 * ROWS, 2 * ROWS)
    angles = 2 * math.pi / NY * order[None, :, None, None] * two[None, None, :, None]
    angles = np.broadcast_to(angles, (PLANES, HALF, 2, NZ)).reshape(ROWS, LANES)
    twiddle = np.stack([np.cos(angles), np.sin(angles)])
    depth = turn(2 * math.pi * (np.outer(full, full) % NZ) / NZ, -1)
    signs = np.array([[1.0, 1.0], [1.0, -1.0]])
    second = np.einsum("dckz,hb->cbzdhk", depth, signs).reshape(2 * LANES, 2 * LANES)
    term = 2.0 - 2.0 * np.cos(2 * math.pi * full / 64)
    excess = term[:, None] + term[None, :] + SCREENING
    kappa = 2.0 * np.arcsinh(0.5 * np.sqrt(excess))
    kappa = kappa.reshape(2, HALF, NZ).transpose(1, 0, 2).reshape(HALF, LANES)
    green = 1.0 / (2.0 * np.sinh(kappa)) / (NY * NZ)
    green[0, 0] = 0.0
    decay = np.stack([np.exp(-kappa * n)[order] for n in (1, 2, 3)])
    step = np.exp(-PLANES * kappa)
    close = 1.0 / (1.0 - np.exp(-NX * kappa))
    near = green * np.exp(-kappa)
    parts = np.stack([step, close, near]).reshape(3, PARTS, 1, 2, LANES)
    parts = np.broadcast_to(parts, (3, PARTS, 4, 2, LANES)).transpose(1, 0, 2, 3, 4).reshape(PARTS, 3, 8, LANES)
    line = np.array([0.0] + [1.0 / (t + SCREENING) for t in term[1:]])
    along = np.cos(2 * math.pi * (np.outer(full, full) % NX) / NX) @ line / NX / (NY * NZ)
    lag = along[(full[:, None] - full[None, :]) % NX].reshape(PARTS, PLANES, PARTS, PLANES)
    uniform = np.zeros((PARTS, 8, PARTS, 8))
    uniform[:, :PLANES, :, :PLANES] = lag
    uniform = uniform.reshape(LANES, LANES)
    columns = turn(2 * math.pi * (np.outer(full, order) % NY) / NY, 1)
    third = np.einsum("dcyk,vx->dvycxk", columns, eye_x).reshape(512, 256)
    back = turn(2 * math.pi * (np.outer(full, full) % NZ) / NZ, 1)
    fourth = np.einsum("dczk,h->chkdz", back, np.ones(2)).reshape(256, 128)
    parity = np.ones((NY, 2, NZ))
    parity[1::2, 1] = -1.0
    parity = np.tile(parity.reshape(NY, LANES), (PLANES, 1))
    names = ("first", "twiddle", "second", "green", "decay", "parts", "uniform", "third", "fourth", "parity")
    values = (first, twiddle, second, green[order], decay, parts, uniform, third, fourth, parity)
    return {n: np.ascontiguousarray(v, dtype=np.float32) for n, v in zip(names, values)}


def dot(a, b):
    return jnp.dot(a, b, precision=lax.Precision.HIGHEST, preferred_element_type=jnp.float32)


def halves(values):
    top = values.astype(jnp.bfloat16)
    return top, (values - top.astype(jnp.float32)).astype(jnp.bfloat16)


def dot_halves(a, b):
    def product(x, y):
        return jnp.dot(x, y, preferred_element_type=jnp.float32)

    return product(a[0], b[0]) + (product(a[0], b[1]) + product(a[1], b[0]))


def density_spectra(electrons, holes, first, twiddle, second):
    real = jnp.zeros((ROWS, LANES), jnp.float32)
    imag = jnp.zeros((ROWS, LANES), jnp.float32)
    for band in range(electrons.shape[0]):
        e_re = electrons[band, 0].astype(jnp.float32)
        e_im = electrons[band, 1].astype(jnp.float32)
        h_re = holes[band, 0].astype(jnp.float32)
        h_im = holes[band, 1].astype(jnp.float32)
        real += e_re * h_re + e_im * h_im
        imag += e_re * h_im - e_im * h_re
    mixed = dot(first[...], jnp.concatenate([real, imag], axis=0))
    u_re, u_im = mixed[:ROWS], mixed[ROWS:]
    t_re = u_re * twiddle[0] + u_im * twiddle[1]
    t_im = u_im * twiddle[0] - u_re * twiddle[1]
    return dot(jnp.concatenate([t_re, t_im], axis=1), second[...])


def planes_of(spectra, c):
    return [spectra[x * HALF : (x + 1) * HALF, c * LANES : (c + 1) * LANES] for x in range(PLANES)]


def moments(spectra, decay):
    found = [[None, None], [None, None]]
    for c in range(2):
        planes = planes_of(spectra, c)
        for way, run in enumerate((planes, planes[::-1])):
            total = run[0]
            for plane in run[1:]:
                total = total * decay + plane
            found[way][c] = total
    return found


def own_kernel(rank, order, electrons, holes, first, twiddle, second, decay, parts, uniform, spectra, sums, mask, part, line):
    values = density_spectra(electrons, holes, first, twiddle, second)
    spectra[...] = values
    found = moments(values, decay[0])
    for way in range(2):
        for c in range(2):
            sums[way * 2 + c] = found[way][c]
    mask[...] = jnp.full((8, LANES), order[0, 0], jnp.int32)
    me = rank[0]
    part[...] = parts[me]
    line[...] = uniform[pl.ds(pl.multiple_of(me * 8, 8), 8), :]


def straight_of(mask, rows):
    return jnp.broadcast_to(mask[0:1], (rows, LANES)) == 0


def far_kernel(mask, electrons, holes, own, first, twiddle, second, decay, spectra, out):
    values = density_spectra(electrons, holes, first, twiddle, second)
    spectra[...] = values
    found = moments(values, decay[0])
    straight = straight_of(mask, HALF)
    for way in range(2):
        for c in range(2):
            near, far = own[way * 2 + c], found[way][c]
            pair = (jnp.where(straight, near, far), jnp.where(straight, far, near))
            for p in range(2):
                for kl in range(2):
                    row = way * 8 + p * 4 + c * 2 + kl
                    out[pl.ds(row, PARTS, stride=16), :] = pair[p][kl * PARTS : (kl + 1) * PARTS]


def total(values):
    return jnp.sum(values, axis=0, keepdims=True)


def local_kernel(mask, own, far, green, decay, local, tail):
    straight = straight_of(mask, HALF)
    weight = [green[...]] + [green[...] * decay[n] for n in range(3)]
    own_values, far_values = own[...], far[...]
    density, field = {}, {}
    for c in range(2):
        near, distant = planes_of(own_values, c), planes_of(far_values, c)
        for x in range(PLANES):
            density[0, c, x] = jnp.where(straight, near[x], distant[x])
            density[1, c, x] = jnp.where(straight, distant[x], near[x])
    for p in range(2):
        for c in range(2):
            for x in range(PLANES):
                value = weight[0] * density[p, c, x]
                for other in range(PLANES):
                    if other != x:
                        value += weight[abs(x - other)] * density[p, c, other]
                field[p, c, x] = value
                local[p, x * HALF : (x + 1) * HALF, c * LANES : (c + 1) * LANES] = value
    zero = jnp.zeros((HALF, LANES), jnp.float32)
    terms = [zero, zero, zero, zero]
    for x in range(PLANES):
        for c in range(2):
            terms[0] += field[0, c, x] * density[0, c, x]
            terms[1] += field[1, c, x] * density[1, c, x]
            terms[2] += field[0, c, x] * density[1, c, x]
        terms[3] += field[0, 1, x] * density[1, 0, x] - field[0, 0, x] * density[1, 1, x]
    lane = lax.broadcasted_iota(jnp.int32, (1, LANES), 1)
    rows = []
    for x in range(PLANES):
        row = jnp.zeros((1, LANES), jnp.float32)
        for p in range(2):
            for c in range(2):
                value = jnp.broadcast_to(density[p, c, x][0:1, 0:1], (1, LANES))
                row = jnp.where(lane // 32 == p * 2 + c, value, row)
        rows.append(row)
    tail[...] = jnp.concatenate(rows + [total(t) for t in terms], axis=0)


def screen_kernel(block, part, tail, out):
    step, close, near = part[0], part[1], part[2]
    right = [block[s, 0:8] for s in range(PARTS)]
    left = [block[s, 8:16] for s in range(PARTS)]
    from_right, from_left = right[0], left[PARTS - 1]
    for n in range(1, PARTS):
        from_right = from_right * step + right[n]
        from_left = from_left * step + left[PARTS - 1 - n]
    from_right, from_left = from_right * close, from_left * close
    effect = {}
    for n in range(PARTS):
        effect[0, n] = near * from_right
        effect[1, PARTS - 1 - n] = near * from_left
        from_right = from_right * step + right[n]
        from_left = from_left * step + left[PARTS - 1 - n]
    zero = jnp.zeros((8, LANES), jnp.float32)
    same, cross, swapped = zero, zero, zero
    for s in range(PARTS):
        for way, moment in ((0, left[s]), (1, right[s])):
            value = effect[way, s]
            out[s, way * 8 : way * 8 + 8] = value
            turned = jnp.concatenate([moment[4:8], moment[0:4]], axis=0)
            same += value * moment
            cross += value * turned
            swapped += value * jnp.concatenate([moment[6:8], moment[4:6], moment[0:4]], axis=0)
    terms = [
        total(same[0:4]),
        total(same[4:8]),
        total(cross[0:4]),
        total(swapped[2:4]) - total(swapped[0:2]),
    ]
    ends = tail[...] + jnp.concatenate([jnp.zeros((4, LANES), jnp.float32)] + terms, axis=0)
    out[:, 16:24] = jnp.broadcast_to(ends[None], (PARTS, 8, LANES))


def field_kernel(block, local, decay, third, fourth, parity, uniform, line, potential, coulomb):
    weight = [None, decay[0], decay[1], decay[2]]

    def effect(way, p, c):
        rows = [block[pl.ds(way * 8 + p * 4 + c * 2 + kl, PARTS, stride=24), :] for kl in range(2)]
        return jnp.concatenate(rows, axis=0)

    columns = []
    for p in range(2):
        planes = []
        for c in range(2):
            right, left = effect(0, p, c), effect(1, p, c)
            for x in range(PLANES):
                value = local[p, x * HALF : (x + 1) * HALF, c * LANES : (c + 1) * LANES]
                value += right if x == 0 else right * weight[x]
                value += left if x == PLANES - 1 else left * weight[PLANES - 1 - x]
                planes.append(value)
        columns.append(jnp.concatenate(planes, axis=0))
    mixed = dot_halves((third[0], third[1]), halves(jnp.concatenate(columns, axis=1)))
    ends = jnp.concatenate([block[pl.ds(24 * s + 16, 8), :] for s in range(PARTS)], axis=0)
    row = lax.broadcasted_iota(jnp.int32, (LANES, LANES), 0)
    plane = jnp.where(row % 8 < PLANES, ends, 0.0)
    plane = jnp.where(row % 8 < PLANES, plane - total(plane) * (1.0 / NX), 0.0)
    own = dot(line[...], plane)
    lane = lax.broadcasted_iota(jnp.int32, (8, LANES), 1)
    by_32, by_64, by_96 = (pltpu.roll(own, n, 1) for n in (32, 64, 96))
    shift = (
        jnp.where(lane < 32, own, jnp.where(lane < 96, by_32, by_64)),
        jnp.where(lane < 32, by_64, jnp.where(lane < 96, by_96, own)),
    )
    signs = parity[...]
    for p in range(2):
        values = mixed[:, p * LANES : (p + 1) * LANES]
        values = jnp.concatenate([values[:256] * signs, values[256:] * signs], axis=1)
        values = dot_halves(halves(values), (fourth[0], fourth[1]))
        for x in range(PLANES):
            potential[p, x] = values[x * NY : (x + 1) * NY] + shift[p][x : x + 1]
    level = dot(uniform[...], plane)
    lane = lax.broadcasted_iota(jnp.int32, (1, LANES), 1)
    same = total(level * plane) * (1.0 / 32)
    cross = total(level * pltpu.roll(plane, 64, 1)) * (1.0 / 32)
    swapped = total(jnp.where(lane < 32, -level * pltpu.roll(plane, 32, 1), level * pltpu.roll(plane, 96, 1))) * (1.0 / 32)
    ahead = lane < 64
    extra = [jnp.where(ahead, same, 0.0), jnp.where(ahead, 0.0, same), jnp.where(ahead, cross, 0.0), jnp.where(ahead, swapped, 0.0)]
    sums = ends[0:8]
    for s in range(1, PARTS):
        sums += ends[s * 8 : s * 8 + 8]
    sums = jnp.sum(sums[4:8] + jnp.concatenate(extra, axis=0), axis=1, keepdims=True) * (1.0 / CELLS)
    c00, c11, re, im = (sums[k : k + 1] for k in range(4))
    row = lax.broadcasted_iota(jnp.int32, (2, 2), 0)
    col = lax.broadcasted_iota(jnp.int32, (2, 2), 1)
    coulomb[0] = jnp.where(row == col, jnp.where(row == 0, c00, c11), re)
    coulomb[1] = jnp.where(row == col, 0.0, jnp.where(row == 0, im, -im))


def full(memory_space=pltpu.VMEM):
    return pl.BlockSpec(memory_space=memory_space)


def call(kernel, name, out_shape, *operands, scalars=0):
    specs = [full(pltpu.SMEM)] * scalars + [full()] * (len(operands) - scalars)
    several = isinstance(out_shape, (list, tuple))
    return pl.pallas_call(
        kernel,
        out_shape=out_shape,
        in_specs=specs,
        out_specs=[full()] * len(out_shape) if several else full(),
        compiler_params=pltpu.CompilerParams(vmem_limit_bytes=32 * 1024 * 1024),
        name=name,
    )(*operands)


def shape(*dims, dtype=jnp.float32):
    return jax.ShapeDtypeStruct(dims, dtype)


def tiled_states(states):
    bands = states.shape[1]
    parts = states.reshape(bands, 2, PLANES, HALF, LANES)
    return parts.transpose(0, 1, 3, 2, 4).reshape(bands, 2, ROWS, LANES)


def split_table(values):
    top = values.astype(ml_dtypes.bfloat16)
    rest = (values - top.astype(np.float32)).astype(ml_dtypes.bfloat16)
    return jnp.asarray(np.stack([top, rest]))


def shards(electrons, holes, pair_order):
    found = tables()
    t = {name: jnp.asarray(value) for name, value in found.items()}
    third, fourth = split_table(found["third"]), split_table(found["fourth"])
    groups = lax.axis_size("blk")
    rank = lax.axis_index("space").astype(jnp.int32).reshape(1)
    previous = lax.ppermute(holes, "blk", [((i - 1) % groups, i) for i in range(groups)])
    e = tiled_states(electrons)
    spectra = shape(ROWS, 2 * LANES)
    own, sums, mask, part, line = call(
        own_kernel, "own_pair",
        [spectra, shape(4, HALF, LANES), shape(8, LANES, dtype=jnp.int32), shape(3, 8, LANES), shape(8, LANES)],
        rank, pair_order, e, tiled_states(holes), t["first"], t["twiddle"], t["second"], t["decay"], t["parts"], t["uniform"],
        scalars=2,
    )
    far, sent = call(
        far_kernel, "far_pair", [spectra, shape(PARTS * 16, LANES)],
        mask, e, tiled_states(previous), sums, t["first"], t["twiddle"], t["second"], t["decay"],
    )
    blocks = lax.all_to_all(sent.reshape(PARTS, 16, LANES), "space", split_axis=0, concat_axis=0, tiled=True)
    local, tail = call(
        local_kernel, "local", [shape(2, ROWS, 2 * LANES), shape(8, LANES)], mask, own, far, t["green"], t["decay"]
    )
    effects = call(screen_kernel, "screen", shape(PARTS, 24, LANES), blocks, part, tail)
    effects = lax.all_to_all(effects, "space", split_axis=0, concat_axis=0, tiled=True)
    potential, coulomb = call(
        field_kernel, "field", [shape(2, PLANES, NY, LANES), shape(2, 2, 2)],
        effects.reshape(PARTS * 24, LANES), local, t["decay"], third, fourth, t["parity"], t["uniform"], line,
    )
    return (potential[None], coulomb[None])


def solution(mesh):
    in_specs = (
        P("blk", None, None, "space", None),
        P("blk", None, None, "space", None),
        P("blk", None),
    )
    out_specs = (P("blk", None, "space", None, None), P("blk", None, None, None))
    return jax.shard_map(shards, mesh=mesh, in_specs=in_specs, out_specs=out_specs, check_vma=False)
```

```python
import math

import jax
import jax.numpy as jnp
import ml_dtypes
import numpy as np
from jax import lax
from jax.experimental import pallas as pl
from jax.experimental.pallas import tpu as pltpu
from jax.sharding import PartitionSpec as P

NX = 64
NY = 64
NZ = 64
CELLS = NX * NY * NZ
SCREENING = 0.01
PARTS = 16
PLANES = NX // PARTS
HALF = NY // 2
ROWS = HALF * PLANES
LANES = 128


def turn(angles, sign):
    cosines, sines = np.cos(angles), sign * np.sin(angles)
    return np.array([[cosines, -sines], [sines, cosines]])


def tables():
    half, full = np.arange(HALF), np.arange(NY)
    two = np.arange(2)
    eye_x = np.eye(PLANES)
    order = np.array([2 * d + kl for kl in range(2) for d in range(PARTS)])
    rows = turn(2 * math.pi * (np.outer(order, half) % HALF) / HALF, -1)
    first = np.einsum("dckn,yx->dykcnx", rows, eye_x).reshape(2 * ROWS, 2 * ROWS)
    angles = 2 * math.pi / NY * order[None, :, None, None] * two[None, None, :, None]
    angles = np.broadcast_to(angles, (PLANES, HALF, 2, NZ)).reshape(ROWS, LANES)
    twiddle = np.stack([np.cos(angles), np.sin(angles)])
    depth = turn(2 * math.pi * (np.outer(full, full) % NZ) / NZ, -1)
    signs = np.array([[1.0, 1.0], [1.0, -1.0]])
    second = np.einsum("dckz,hb->cbzdhk", depth, signs).reshape(2 * LANES, 2 * LANES)
    term = 2.0 - 2.0 * np.cos(2 * math.pi * full / 64)
    excess = term[:, None] + term[None, :] + SCREENING
    kappa = 2.0 * np.arcsinh(0.5 * np.sqrt(excess))
    kappa = kappa.reshape(2, HALF, NZ).transpose(1, 0, 2).reshape(HALF, LANES)
    green = 1.0 / (2.0 * np.sinh(kappa)) / (NY * NZ)
    green[0, 0] = 0.0
    decay = np.stack([np.exp(-kappa * n)[order] for n in (1, 2, 3)])
    step = np.exp(-PLANES * kappa)
    close = 1.0 / (1.0 - np.exp(-NX * kappa))
    near = green * np.exp(-kappa)
    parts = np.stack([step, close, near]).reshape(3, PARTS, 1, 2, LANES)
    parts = np.broadcast_to(parts, (3, PARTS, 4, 2, LANES)).transpose(1, 0, 2, 3, 4).reshape(PARTS, 3, 8, LANES)
    line = np.array([0.0] + [1.0 / (t + SCREENING) for t in term[1:]])
    along = np.cos(2 * math.pi * (np.outer(full, full) % NX) / NX) @ line / NX / (NY * NZ)
    lag = along[(full[:, None] - full[None, :]) % NX].reshape(PARTS, PLANES, PARTS, PLANES)
    uniform = np.zeros((PARTS, 8, PARTS, 8))
    uniform[:, :PLANES, :, :PLANES] = lag
    uniform = uniform.reshape(PARTS, 8, LANES)
    back = turn(2 * math.pi * (np.outer(full, full) % NZ) / NZ, 1)
    third = np.einsum("dczk,hb->chkdbz", back, signs).reshape(2 * LANES, 2 * LANES)
    columns = turn(2 * math.pi * (np.outer(half, order) % HALF) / HALF, 1)
    fourth = np.einsum("dcnk,yx->dyncxk", columns, eye_x).reshape(2 * ROWS, 2 * ROWS)
    names = ("first", "twiddle", "second", "green", "decay", "parts", "uniform", "third", "fourth")
    values = (first, twiddle, second, green[order], decay, parts, uniform, third, fourth)
    return {n: np.ascontiguousarray(v, dtype=np.float32) for n, v in zip(names, values)}


def dot(a, b):
    return jnp.dot(a, b, precision=lax.Precision.HIGHEST, preferred_element_type=jnp.float32)


def halves(values):
    top = values.astype(jnp.bfloat16)
    return top, (values - top.astype(jnp.float32)).astype(jnp.bfloat16)


def dot_halves(a, b):
    def product(x, y):
        return jnp.dot(x, y, preferred_element_type=jnp.float32)

    return product(a[0], b[0]) + (product(a[0], b[1]) + product(a[1], b[0]))


def density_spectra(electrons, holes, first, twiddle, second):
    real = jnp.zeros((ROWS, LANES), jnp.float32)
    imag = jnp.zeros((ROWS, LANES), jnp.float32)
    for band in range(electrons.shape[0]):
        e_re = electrons[band, 0].astype(jnp.float32)
        e_im = electrons[band, 1].astype(jnp.float32)
        h_re = holes[band, 0].astype(jnp.float32)
        h_im = holes[band, 1].astype(jnp.float32)
        real += e_re * h_re + e_im * h_im
        imag += e_re * h_im - e_im * h_re
    mixed = dot(first[...], jnp.concatenate([real, imag], axis=0))
    u_re, u_im = mixed[:ROWS], mixed[ROWS:]
    t_re = u_re * twiddle[0] + u_im * twiddle[1]
    t_im = u_im * twiddle[0] - u_re * twiddle[1]
    return dot(jnp.concatenate([t_re, t_im], axis=1), second[...])


def planes_of(spectra, c):
    return [spectra[x * HALF : (x + 1) * HALF, c * LANES : (c + 1) * LANES] for x in range(PLANES)]


def moments(spectra, decay):
    found = [[None, None], [None, None]]
    for c in range(2):
        planes = planes_of(spectra, c)
        for way, run in enumerate((planes, planes[::-1])):
            total = run[0]
            for plane in run[1:]:
                total = total * decay + plane
            found[way][c] = total
    return found


def own_kernel(rank, order, *refs):
    sources, (spectra, sums, mask, part, line) = refs[:8], refs[8:13]
    copies, sems = refs[13:19], refs[19]
    me = rank[0]
    sources = sources[:6] + (sources[6].at[me], sources[7].at[me])
    moves = [
        pltpu.make_async_copy(source, target, sems.at[n])
        for n, (source, target) in enumerate(zip(sources, copies + (part, line)))
    ]
    for move in moves:
        move.start()
    mask[...] = jnp.full((8, LANES), order[0, 0], jnp.int32)
    for move in moves:
        move.wait()
    electrons, holes, first, second, twiddle, decay = copies
    values = density_spectra(electrons, holes, first, twiddle, second)
    spectra[...] = values
    found = moments(values, decay[0])
    for way in range(2):
        for c in range(2):
            sums[way * 2 + c] = found[way][c]


def straight_of(mask, rows):
    return jnp.broadcast_to(mask[0:1], (rows, LANES)) == 0


def far_kernel(mask, electrons, holes, own, first, twiddle, second, decay, spectra, out):
    values = density_spectra(electrons, holes, first, twiddle, second)
    spectra[...] = values
    found = moments(values, decay[0])
    straight = straight_of(mask, HALF)
    for way in range(2):
        for c in range(2):
            near, far = own[way * 2 + c], found[way][c]
            pair = (jnp.where(straight, near, far), jnp.where(straight, far, near))
            for p in range(2):
                for kl in range(2):
                    row = way * 8 + p * 4 + c * 2 + kl
                    out[pl.ds(row, PARTS, stride=16), :] = pair[p][kl * PARTS : (kl + 1) * PARTS]


def total(values):
    return jnp.sum(values, axis=0, keepdims=True)


def local_terms(mask, own, far, green, decay, local):
    straight = straight_of(mask, HALF)
    weight = [green[...]] + [green[...] * decay[n] for n in range(3)]
    own_values, far_values = own[...], far[...]
    density, field = {}, {}
    for c in range(2):
        near, distant = planes_of(own_values, c), planes_of(far_values, c)
        for x in range(PLANES):
            density[0, c, x] = jnp.where(straight, near[x], distant[x])
            density[1, c, x] = jnp.where(straight, distant[x], near[x])
    for p in range(2):
        for c in range(2):
            for x in range(PLANES):
                value = weight[0] * density[p, c, x]
                for other in range(PLANES):
                    if other != x:
                        value += weight[abs(x - other)] * density[p, c, other]
                field[p, c, x] = value
                local[p, x * HALF : (x + 1) * HALF, c * LANES : (c + 1) * LANES] = value
    zero = jnp.zeros((HALF, LANES), jnp.float32)
    terms = [zero, zero, zero, zero]
    for x in range(PLANES):
        for c in range(2):
            terms[0] += field[0, c, x] * density[0, c, x]
            terms[1] += field[1, c, x] * density[1, c, x]
            terms[2] += field[0, c, x] * density[1, c, x]
        terms[3] += field[0, 1, x] * density[1, 0, x] - field[0, 0, x] * density[1, 1, x]
    lane = lax.broadcasted_iota(jnp.int32, (1, LANES), 1)
    rows = []
    for x in range(PLANES):
        row = jnp.zeros((1, LANES), jnp.float32)
        for p in range(2):
            for c in range(2):
                value = jnp.broadcast_to(density[p, c, x][0:1, 0:1], (1, LANES))
                row = jnp.where(lane // 32 == p * 2 + c, value, row)
        rows.append(row)
    return jnp.concatenate(rows + [total(t) for t in terms], axis=0)


def screen_kernel(block, part, mask, own, far, green, decay, out, local):
    tail = local_terms(mask, own, far, green, decay, local)
    step, close, near = part[0], part[1], part[2]
    right = [block[s, 0:8] for s in range(PARTS)]
    left = [block[s, 8:16] for s in range(PARTS)]
    from_right, from_left = right[0], left[PARTS - 1]
    for n in range(1, PARTS):
        from_right = from_right * step + right[n]
        from_left = from_left * step + left[PARTS - 1 - n]
    from_right, from_left = from_right * close, from_left * close
    effect = {}
    for n in range(PARTS):
        effect[0, n] = near * from_right
        effect[1, PARTS - 1 - n] = near * from_left
        from_right = from_right * step + right[n]
        from_left = from_left * step + left[PARTS - 1 - n]
    zero = jnp.zeros((8, LANES), jnp.float32)
    same, cross, swapped = zero, zero, zero
    for s in range(PARTS):
        for way, moment in ((0, left[s]), (1, right[s])):
            value = effect[way, s]
            out[s, way * 8 : way * 8 + 8] = value
            turned = jnp.concatenate([moment[4:8], moment[0:4]], axis=0)
            same += value * moment
            cross += value * turned
            swapped += value * jnp.concatenate([moment[6:8], moment[4:6], moment[0:4]], axis=0)
    terms = [
        total(same[0:4]),
        total(same[4:8]),
        total(cross[0:4]),
        total(swapped[2:4]) - total(swapped[0:2]),
    ]
    ends = tail + jnp.concatenate([jnp.zeros((4, LANES), jnp.float32)] + terms, axis=0)
    out[:, 16:24] = jnp.broadcast_to(ends[None], (PARTS, 8, LANES))


def field_kernel(block, local, decay, twiddle, third, fourth, uniform, line, potential, coulomb):
    weight = [None, decay[0], decay[1], decay[2]]

    def effect(way, p, c):
        rows = [block[pl.ds(way * 8 + p * 4 + c * 2 + kl, PARTS, stride=24), :] for kl in range(2)]
        return jnp.concatenate(rows, axis=0)

    pairs = []
    for p in range(2):
        parts = []
        for c in range(2):
            right, left = effect(0, p, c), effect(1, p, c)
            planes = []
            for x in range(PLANES):
                value = local[p, x * HALF : (x + 1) * HALF, c * LANES : (c + 1) * LANES]
                value += right if x == 0 else right * weight[x]
                value += left if x == PLANES - 1 else left * weight[PLANES - 1 - x]
                planes.append(value)
            parts.append(jnp.concatenate(planes, axis=0))
        pairs.append(jnp.concatenate(parts, axis=1))
    mixed = dot_halves(halves(jnp.concatenate(pairs, axis=0)), (third[0], third[1]))
    columns = []
    for p in range(2):
        u_re, u_im = mixed[p * ROWS : (p + 1) * ROWS, :LANES], mixed[p * ROWS : (p + 1) * ROWS, LANES:]
        t_re = u_re * twiddle[0] - u_im * twiddle[1]
        t_im = u_im * twiddle[0] + u_re * twiddle[1]
        columns.append(jnp.concatenate([t_re, t_im], axis=0))
    ends = jnp.concatenate([block[pl.ds(24 * s + 16, 8), :] for s in range(PARTS)], axis=0)
    row = lax.broadcasted_iota(jnp.int32, (LANES, LANES), 0)
    plane = jnp.where(row % 8 < PLANES, ends, 0.0)
    plane = jnp.where(row % 8 < PLANES, plane - total(plane) * (1.0 / NX), 0.0)
    own = dot(line[...], plane)
    lane = lax.broadcasted_iota(jnp.int32, (8, LANES), 1)
    by_32, by_64, by_96 = (pltpu.roll(own, n, 1) for n in (32, 64, 96))
    shift = (
        jnp.where(lane < 32, own, jnp.where(lane < 96, by_32, by_64)),
        jnp.where(lane < 32, by_64, jnp.where(lane < 96, by_96, own)),
    )
    lane = lax.broadcasted_iota(jnp.int32, (HALF, LANES), 1)
    for p in range(2):
        values = dot_halves((fourth[0], fourth[1]), halves(columns[p]))
        for x in range(PLANES):
            re, im = values[x * HALF : (x + 1) * HALF], values[ROWS + x * HALF : ROWS + (x + 1) * HALF]
            even = jnp.where(lane < NZ, re, pltpu.roll(im, NZ, 1))
            odd = jnp.where(lane < NZ, pltpu.roll(re, NZ, 1), im)
            potential[p, x, pl.ds(0, HALF, stride=2), :] = even + shift[p][x : x + 1]
            potential[p, x, pl.ds(1, HALF, stride=2), :] = odd + shift[p][x : x + 1]
    level = dot(uniform[...].reshape(LANES, LANES), plane)
    lane = lax.broadcasted_iota(jnp.int32, (1, LANES), 1)
    same = total(level * plane) * (1.0 / 32)
    cross = total(level * pltpu.roll(plane, 64, 1)) * (1.0 / 32)
    swapped = total(jnp.where(lane < 32, -level * pltpu.roll(plane, 32, 1), level * pltpu.roll(plane, 96, 1))) * (1.0 / 32)
    ahead = lane < 64
    extra = [jnp.where(ahead, same, 0.0), jnp.where(ahead, 0.0, same), jnp.where(ahead, cross, 0.0), jnp.where(ahead, swapped, 0.0)]
    sums = ends[0:8]
    for s in range(1, PARTS):
        sums += ends[s * 8 : s * 8 + 8]
    sums = jnp.sum(sums[4:8] + jnp.concatenate(extra, axis=0), axis=1, keepdims=True) * (1.0 / CELLS)
    c00, c11, re, im = (sums[k : k + 1] for k in range(4))
    row = lax.broadcasted_iota(jnp.int32, (2, 2), 0)
    col = lax.broadcasted_iota(jnp.int32, (2, 2), 1)
    coulomb[0] = jnp.where(row == col, jnp.where(row == 0, c00, c11), re)
    coulomb[1] = jnp.where(row == col, 0.0, jnp.where(row == 0, im, -im))


def full(memory_space=pltpu.VMEM):
    return pl.BlockSpec(memory_space=memory_space)


def call(kernel, name, out_shape, *operands, scalars=0, space=pltpu.VMEM, scratch=(), limit=32):
    specs = [full(pltpu.SMEM)] * scalars + [full(space)] * (len(operands) - scalars)
    several = isinstance(out_shape, (list, tuple))
    return pl.pallas_call(
        kernel,
        out_shape=out_shape,
        in_specs=specs,
        out_specs=[full()] * len(out_shape) if several else full(),
        scratch_shapes=scratch,
        compiler_params=pltpu.CompilerParams(vmem_limit_bytes=limit * 1024 * 1024),
        name=name,
    )(*operands)


def shape(*dims, dtype=jnp.float32):
    return jax.ShapeDtypeStruct(dims, dtype)


def tiled_states(states):
    bands = states.shape[1]
    parts = states.reshape(bands, 2, PLANES, HALF, LANES)
    return parts.transpose(0, 1, 3, 2, 4).reshape(bands, 2, ROWS, LANES)


def split_table(values):
    top = values.astype(ml_dtypes.bfloat16)
    rest = (values - top.astype(np.float32)).astype(ml_dtypes.bfloat16)
    return jnp.asarray(np.stack([top, rest]))


def shards(electrons, holes, pair_order):
    found = tables()
    t = {name: jnp.asarray(value) for name, value in found.items()}
    third, fourth = split_table(found["third"]), split_table(found["fourth"])
    groups = lax.axis_size("blk")
    rank = lax.axis_index("space").astype(jnp.int32).reshape(1)
    previous = lax.ppermute(holes, "blk", [((i - 1) % groups, i) for i in range(groups)])
    e = tiled_states(electrons)
    spectra = shape(ROWS, 2 * LANES)
    h = tiled_states(holes)
    brought = (e, h, t["first"], t["second"], t["twiddle"], t["decay"])
    own, sums, mask, part, line = call(
        own_kernel, "own_pair",
        [spectra, shape(4, HALF, LANES), shape(8, LANES, dtype=jnp.int32), shape(3, 8, LANES), shape(8, LANES)],
        rank, pair_order, *brought, t["parts"], t["uniform"],
        scalars=2, space=pltpu.HBM, limit=60,
        scratch=[pltpu.VMEM(x.shape, x.dtype) for x in brought] + [pltpu.SemaphoreType.DMA((8,))],
    )
    far, sent = call(
        far_kernel, "far_pair", [spectra, shape(PARTS * 16, LANES)],
        mask, e, tiled_states(previous), sums, t["first"], t["twiddle"], t["second"], t["decay"],
    )
    blocks = lax.all_to_all(sent.reshape(PARTS, 16, LANES), "space", split_axis=0, concat_axis=0, tiled=True)
    effects, local = call(
        screen_kernel, "screen", [shape(PARTS, 24, LANES), shape(2, ROWS, 2 * LANES)],
        blocks, part, mask, own, far, t["green"], t["decay"],
    )
    effects = lax.all_to_all(effects, "space", split_axis=0, concat_axis=0, tiled=True)
    potential, coulomb = call(
        field_kernel, "field", [shape(2, PLANES, NY, LANES), shape(2, 2, 2)],
        effects.reshape(PARTS * 24, LANES), local, t["decay"], t["twiddle"], third, fourth, t["uniform"], line,
    )
    return (potential[None], coulomb[None])


def solution(mesh):
    in_specs = (
        P("blk", None, None, "space", None),
        P("blk", None, None, "space", None),
        P("blk", None),
    )
    out_specs = (P("blk", None, "space", None, None), P("blk", None, None, None))
    return jax.shard_map(shards, mesh=mesh, in_specs=in_specs, out_specs=out_specs, check_vma=False)
```

```python
import math

import jax
import jax.numpy as jnp
import ml_dtypes
import numpy as np
from jax import lax
from jax.experimental import pallas as pl
from jax.experimental.pallas import tpu as pltpu
from jax.sharding import PartitionSpec as P

NX = 64
NY = 64
NZ = 64
CELLS = NX * NY * NZ
SCREENING = 0.01
PARTS = 16
PLANES = NX // PARTS
HALF = NY // 2
ROWS = HALF * PLANES
LANES = 128


def turn(angles, sign):
    cosines, sines = np.cos(angles), sign * np.sin(angles)
    return np.array([[cosines, -sines], [sines, cosines]])


def tables():
    half, full = np.arange(HALF), np.arange(NY)
    two = np.arange(2)
    eye_x = np.eye(PLANES)
    order = np.array([2 * d + kl for kl in range(2) for d in range(PARTS)])
    rows = turn(2 * math.pi * (np.outer(order, half) % HALF) / HALF, -1)
    first = np.einsum("dckn,yx->dykcnx", rows, eye_x).reshape(2 * ROWS, 2 * ROWS)
    angles = 2 * math.pi / NY * order[None, :, None, None] * two[None, None, :, None]
    angles = np.broadcast_to(angles, (PLANES, HALF, 2, NZ)).reshape(ROWS, LANES)
    twiddle = np.stack([np.cos(angles), np.sin(angles)])
    depth = turn(2 * math.pi * (np.outer(full, full) % NZ) / NZ, -1)
    signs = np.array([[1.0, 1.0], [1.0, -1.0]])
    second = np.einsum("dckz,hb->cbzdhk", depth, signs).reshape(2 * LANES, 2 * LANES)
    term = 2.0 - 2.0 * np.cos(2 * math.pi * full / 64)
    excess = term[:, None] + term[None, :] + SCREENING
    kappa = 2.0 * np.arcsinh(0.5 * np.sqrt(excess))
    kappa = kappa.reshape(2, HALF, NZ).transpose(1, 0, 2).reshape(HALF, LANES)
    green = 1.0 / (2.0 * np.sinh(kappa)) / (NY * NZ)
    green[0, 0] = 0.0
    decay = np.stack([np.exp(-kappa * n)[order] for n in (1, 2, 3)])
    step = np.exp(-PLANES * kappa)
    close = 1.0 / (1.0 - np.exp(-NX * kappa))
    near = green * np.exp(-kappa)
    parts = np.stack([step, close, near]).reshape(3, PARTS, 1, 2, LANES)
    parts = np.broadcast_to(parts, (3, PARTS, 4, 2, LANES)).transpose(1, 0, 2, 3, 4).reshape(PARTS, 3, 8, LANES)
    line = np.array([0.0] + [1.0 / (t + SCREENING) for t in term[1:]])
    along = np.cos(2 * math.pi * (np.outer(full, full) % NX) / NX) @ line / NX / (NY * NZ)
    lag = along[(full[:, None] - full[None, :]) % NX].reshape(PARTS, PLANES, PARTS, PLANES)
    uniform = np.zeros((PARTS, 8, PARTS, 8))
    uniform[:, :PLANES, :, :PLANES] = lag
    uniform = uniform.reshape(PARTS, 8, LANES)
    back = turn(2 * math.pi * (np.outer(full, full) % NZ) / NZ, 1)
    third = np.einsum("dczk,hb->chkdbz", back, signs).reshape(2 * LANES, 2 * LANES)
    columns = turn(2 * math.pi * (np.outer(half, order) % HALF) / HALF, 1)
    fourth = np.einsum("dcnk,yx->dyncxk", columns, eye_x).reshape(2 * ROWS, 2 * ROWS)
    names = ("first", "twiddle", "second", "green", "decay", "parts", "uniform", "third", "fourth")
    values = (first, twiddle, second, green[order], decay, parts, uniform, third, fourth)
    return {n: np.ascontiguousarray(v, dtype=np.float32) for n, v in zip(names, values)}


def dot(a, b):
    return jnp.dot(a, b, precision=lax.Precision.HIGHEST, preferred_element_type=jnp.float32)


def halves(values):
    top = values.astype(jnp.bfloat16)
    return top, (values - top.astype(jnp.float32)).astype(jnp.bfloat16)


def dot_halves(a, b):
    def product(x, y):
        return jnp.dot(x, y, preferred_element_type=jnp.float32)

    return product(a[0], b[0]) + (product(a[0], b[1]) + product(a[1], b[0]))


def density_spectra(electrons, holes, first, twiddle, second):
    real = jnp.zeros((ROWS, LANES), jnp.float32)
    imag = jnp.zeros((ROWS, LANES), jnp.float32)
    for band in range(electrons.shape[0]):
        e_re = electrons[band, 0].astype(jnp.float32)
        e_im = electrons[band, 1].astype(jnp.float32)
        h_re = holes[band, 0].astype(jnp.float32)
        h_im = holes[band, 1].astype(jnp.float32)
        real += e_re * h_re + e_im * h_im
        imag += e_re * h_im - e_im * h_re
    mixed = dot(first[...], jnp.concatenate([real, imag], axis=0))
    u_re, u_im = mixed[:ROWS], mixed[ROWS:]
    t_re = u_re * twiddle[0] + u_im * twiddle[1]
    t_im = u_im * twiddle[0] - u_re * twiddle[1]
    return dot(jnp.concatenate([t_re, t_im], axis=1), second[...])


def planes_of(spectra, c):
    return [spectra[x * HALF : (x + 1) * HALF, c * LANES : (c + 1) * LANES] for x in range(PLANES)]


def moments(spectra, decay):
    found = [[None, None], [None, None]]
    for c in range(2):
        planes = planes_of(spectra, c)
        for way, run in enumerate((planes, planes[::-1])):
            total = run[0]
            for plane in run[1:]:
                total = total * decay + plane
            found[way][c] = total
    return found


def own_kernel(rank, order, *refs):
    sources, (spectra, sums, mask, part, line) = refs[:8], refs[8:13]
    copies, sems = refs[13:19], refs[19]
    me = rank[0]
    sources = sources[:6] + (sources[6].at[me], sources[7].at[me])
    moves = [
        pltpu.make_async_copy(source, target, sems.at[n])
        for n, (source, target) in enumerate(zip(sources, copies + (part, line)))
    ]
    for move in moves:
        move.start()
    mask[...] = jnp.full((8, LANES), order[0, 0], jnp.int32)
    for move in moves:
        move.wait()
    electrons, holes, first, second, twiddle, decay = copies
    values = density_spectra(electrons, holes, first, twiddle, second)
    spectra[...] = values
    found = moments(values, decay[0])
    for way in range(2):
        for c in range(2):
            sums[way * 2 + c] = found[way][c]


def hold_kernel(*refs):
    for source, target in zip(refs[: len(refs) // 2], refs[len(refs) // 2 :]):
        target[...] = source[...]


def straight_of(mask, rows):
    return jnp.broadcast_to(mask[0:1], (rows, LANES)) == 0


def far_kernel(mask, electrons, holes, own, first, twiddle, second, decay, spectra, out):
    values = density_spectra(electrons, holes, first, twiddle, second)
    spectra[...] = values
    found = moments(values, decay[0])
    straight = straight_of(mask, HALF)
    for way in range(2):
        for c in range(2):
            near, far = own[way * 2 + c], found[way][c]
            pair = (jnp.where(straight, near, far), jnp.where(straight, far, near))
            for p in range(2):
                for kl in range(2):
                    row = way * 8 + p * 4 + c * 2 + kl
                    out[pl.ds(row, PARTS, stride=16), :] = pair[p][kl * PARTS : (kl + 1) * PARTS]


def total(values):
    return jnp.sum(values, axis=0, keepdims=True)


def local_terms(mask, own, far, green, decay, local):
    straight = straight_of(mask, HALF)
    weight = [green[...]] + [green[...] * decay[n] for n in range(3)]
    own_values, far_values = own[...], far[...]
    density, field = {}, {}
    for c in range(2):
        near, distant = planes_of(own_values, c), planes_of(far_values, c)
        for x in range(PLANES):
            density[0, c, x] = jnp.where(straight, near[x], distant[x])
            density[1, c, x] = jnp.where(straight, distant[x], near[x])
    for p in range(2):
        for c in range(2):
            for x in range(PLANES):
                value = weight[0] * density[p, c, x]
                for other in range(PLANES):
                    if other != x:
                        value += weight[abs(x - other)] * density[p, c, other]
                field[p, c, x] = value
                local[p, x * HALF : (x + 1) * HALF, c * LANES : (c + 1) * LANES] = value
    zero = jnp.zeros((HALF, LANES), jnp.float32)
    terms = [zero, zero, zero, zero]
    for x in range(PLANES):
        for c in range(2):
            terms[0] += field[0, c, x] * density[0, c, x]
            terms[1] += field[1, c, x] * density[1, c, x]
            terms[2] += field[0, c, x] * density[1, c, x]
        terms[3] += field[0, 1, x] * density[1, 0, x] - field[0, 0, x] * density[1, 1, x]
    lane = lax.broadcasted_iota(jnp.int32, (1, LANES), 1)
    rows = []
    for x in range(PLANES):
        row = jnp.zeros((1, LANES), jnp.float32)
        for p in range(2):
            for c in range(2):
                value = jnp.broadcast_to(density[p, c, x][0:1, 0:1], (1, LANES))
                row = jnp.where(lane // 32 == p * 2 + c, value, row)
        rows.append(row)
    return jnp.concatenate(rows + [total(t) for t in terms], axis=0)


def screen_kernel(block, part, mask, own, far, green, decay, out, local):
    tail = local_terms(mask, own, far, green, decay, local)
    step, close, near = part[0], part[1], part[2]
    right = [block[s, 0:8] for s in range(PARTS)]
    left = [block[s, 8:16] for s in range(PARTS)]
    from_right, from_left = right[0], left[PARTS - 1]
    for n in range(1, PARTS):
        from_right = from_right * step + right[n]
        from_left = from_left * step + left[PARTS - 1 - n]
    from_right, from_left = from_right * close, from_left * close
    effect = {}
    for n in range(PARTS):
        effect[0, n] = near * from_right
        effect[1, PARTS - 1 - n] = near * from_left
        from_right = from_right * step + right[n]
        from_left = from_left * step + left[PARTS - 1 - n]
    zero = jnp.zeros((8, LANES), jnp.float32)
    same, cross, swapped = zero, zero, zero
    for s in range(PARTS):
        for way, moment in ((0, left[s]), (1, right[s])):
            value = effect[way, s]
            out[s, way * 8 : way * 8 + 8] = value
            turned = jnp.concatenate([moment[4:8], moment[0:4]], axis=0)
            same += value * moment
            cross += value * turned
            swapped += value * jnp.concatenate([moment[6:8], moment[4:6], moment[0:4]], axis=0)
    terms = [
        total(same[0:4]),
        total(same[4:8]),
        total(cross[0:4]),
        total(swapped[2:4]) - total(swapped[0:2]),
    ]
    ends = tail + jnp.concatenate([jnp.zeros((4, LANES), jnp.float32)] + terms, axis=0)
    out[:, 16:24] = jnp.broadcast_to(ends[None], (PARTS, 8, LANES))


def field_kernel(block, local, decay, twiddle, third, fourth, uniform, line, potential, coulomb):
    weight = [None, decay[0], decay[1], decay[2]]

    def effect(way, p, c):
        rows = [block[pl.ds(way * 8 + p * 4 + c * 2 + kl, PARTS, stride=24), :] for kl in range(2)]
        return jnp.concatenate(rows, axis=0)

    pairs = []
    for p in range(2):
        parts = []
        for c in range(2):
            right, left = effect(0, p, c), effect(1, p, c)
            planes = []
            for x in range(PLANES):
                value = local[p, x * HALF : (x + 1) * HALF, c * LANES : (c + 1) * LANES]
                value += right if x == 0 else right * weight[x]
                value += left if x == PLANES - 1 else left * weight[PLANES - 1 - x]
                planes.append(value)
            parts.append(jnp.concatenate(planes, axis=0))
        pairs.append(jnp.concatenate(parts, axis=1))
    mixed = dot_halves(halves(jnp.concatenate(pairs, axis=0)), (third[0], third[1]))
    columns = []
    for p in range(2):
        u_re, u_im = mixed[p * ROWS : (p + 1) * ROWS, :LANES], mixed[p * ROWS : (p + 1) * ROWS, LANES:]
        t_re = u_re * twiddle[0] - u_im * twiddle[1]
        t_im = u_im * twiddle[0] + u_re * twiddle[1]
        columns.append(jnp.concatenate([t_re, t_im], axis=0))
    ends = jnp.concatenate([block[pl.ds(24 * s + 16, 8), :] for s in range(PARTS)], axis=0)
    row = lax.broadcasted_iota(jnp.int32, (LANES, LANES), 0)
    plane = jnp.where(row % 8 < PLANES, ends, 0.0)
    plane = jnp.where(row % 8 < PLANES, plane - total(plane) * (1.0 / NX), 0.0)
    own = dot(line[...], plane)
    lane = lax.broadcasted_iota(jnp.int32, (8, LANES), 1)
    by_32, by_64, by_96 = (pltpu.roll(own, n, 1) for n in (32, 64, 96))
    shift = (
        jnp.where(lane < 32, own, jnp.where(lane < 96, by_32, by_64)),
        jnp.where(lane < 32, by_64, jnp.where(lane < 96, by_96, own)),
    )
    lane = lax.broadcasted_iota(jnp.int32, (HALF, LANES), 1)
    for p in range(2):
        values = dot_halves((fourth[0], fourth[1]), halves(columns[p]))
        for x in range(PLANES):
            re, im = values[x * HALF : (x + 1) * HALF], values[ROWS + x * HALF : ROWS + (x + 1) * HALF]
            even = jnp.where(lane < NZ, re, pltpu.roll(im, NZ, 1))
            odd = jnp.where(lane < NZ, pltpu.roll(re, NZ, 1), im)
            potential[p, x, pl.ds(0, HALF, stride=2), :] = even + shift[p][x : x + 1]
            potential[p, x, pl.ds(1, HALF, stride=2), :] = odd + shift[p][x : x + 1]
    level = dot(uniform[...].reshape(LANES, LANES), plane)
    lane = lax.broadcasted_iota(jnp.int32, (1, LANES), 1)
    same = total(level * plane) * (1.0 / 32)
    cross = total(level * pltpu.roll(plane, 64, 1)) * (1.0 / 32)
    swapped = total(jnp.where(lane < 32, -level * pltpu.roll(plane, 32, 1), level * pltpu.roll(plane, 96, 1))) * (1.0 / 32)
    ahead = lane < 64
    extra = [jnp.where(ahead, same, 0.0), jnp.where(ahead, 0.0, same), jnp.where(ahead, cross, 0.0), jnp.where(ahead, swapped, 0.0)]
    sums = ends[0:8]
    for s in range(1, PARTS):
        sums += ends[s * 8 : s * 8 + 8]
    sums = jnp.sum(sums[4:8] + jnp.concatenate(extra, axis=0), axis=1, keepdims=True) * (1.0 / CELLS)
    c00, c11, re, im = (sums[k : k + 1] for k in range(4))
    row = lax.broadcasted_iota(jnp.int32, (2, 2), 0)
    col = lax.broadcasted_iota(jnp.int32, (2, 2), 1)
    coulomb[0] = jnp.where(row == col, jnp.where(row == 0, c00, c11), re)
    coulomb[1] = jnp.where(row == col, 0.0, jnp.where(row == 0, im, -im))


def full(memory_space=pltpu.VMEM):
    return pl.BlockSpec(memory_space=memory_space)


def call(kernel, name, out_shape, *operands, scalars=0, space=pltpu.VMEM, scratch=(), limit=32):
    specs = [full(pltpu.SMEM)] * scalars + [full(space)] * (len(operands) - scalars)
    several = isinstance(out_shape, (list, tuple))
    return pl.pallas_call(
        kernel,
        out_shape=out_shape,
        in_specs=specs,
        out_specs=[full()] * len(out_shape) if several else full(),
        scratch_shapes=scratch,
        compiler_params=pltpu.CompilerParams(vmem_limit_bytes=limit * 1024 * 1024),
        name=name,
    )(*operands)


def shape(*dims, dtype=jnp.float32):
    return jax.ShapeDtypeStruct(dims, dtype)


def tiled_states(states):
    bands = states.shape[1]
    parts = states.reshape(bands, 2, PLANES, HALF, LANES)
    return parts.transpose(0, 1, 3, 2, 4).reshape(bands, 2, ROWS, LANES)


def split_table(values):
    top = values.astype(ml_dtypes.bfloat16)
    rest = (values - top.astype(np.float32)).astype(ml_dtypes.bfloat16)
    return jnp.asarray(np.stack([top, rest]))


def shards(electrons, holes, pair_order):
    found = tables()
    t = {name: jnp.asarray(value) for name, value in found.items()}
    third, fourth = split_table(found["third"]), split_table(found["fourth"])
    groups = lax.axis_size("blk")
    rank = lax.axis_index("space").astype(jnp.int32).reshape(1)
    previous = lax.ppermute(holes, "blk", [((i - 1) % groups, i) for i in range(groups)])
    e = tiled_states(electrons)
    spectra = shape(ROWS, 2 * LANES)
    h = tiled_states(holes)
    brought = (e, h, t["first"], t["second"], t["twiddle"], t["decay"])
    made = call(
        own_kernel, "own_pair",
        [spectra, shape(4, HALF, LANES), shape(8, LANES, dtype=jnp.int32), shape(3, 8, LANES), shape(8, LANES)],
        rank, pair_order, *brought, t["parts"], t["uniform"],
        scalars=2, space=pltpu.HBM, limit=60,
        scratch=[pltpu.VMEM(x.shape, x.dtype) for x in brought] + [pltpu.SemaphoreType.DMA((8,))],
    )
    own, sums, mask, part, line = call(
        hold_kernel, "hold", [jax.ShapeDtypeStruct(x.shape, x.dtype) for x in made], *made
    )
    far, sent = call(
        far_kernel, "far_pair", [spectra, shape(PARTS * 16, LANES)],
        mask, e, tiled_states(previous), sums, t["first"], t["twiddle"], t["second"], t["decay"],
    )
    blocks = lax.all_to_all(sent.reshape(PARTS, 16, LANES), "space", split_axis=0, concat_axis=0, tiled=True)
    effects, local = call(
        screen_kernel, "screen", [shape(PARTS, 24, LANES), shape(2, ROWS, 2 * LANES)],
        blocks, part, mask, own, far, t["green"], t["decay"],
    )
    effects = lax.all_to_all(effects, "space", split_axis=0, concat_axis=0, tiled=True)
    potential, coulomb = call(
        field_kernel, "field", [shape(2, PLANES, NY, LANES), shape(2, 2, 2)],
        effects.reshape(PARTS * 24, LANES), local, t["decay"], t["twiddle"], third, fourth, t["uniform"], line,
    )
    return (potential[None], coulomb[None])


def solution(mesh):
    in_specs = (
        P("blk", None, None, "space", None),
        P("blk", None, None, "space", None),
        P("blk", None),
    )
    out_specs = (P("blk", None, "space", None, None), P("blk", None, None, None))
    return jax.shard_map(shards, mesh=mesh, in_specs=in_specs, out_specs=out_specs, check_vma=False)
```

```python
import math

import jax
import jax.numpy as jnp
import ml_dtypes
import numpy as np
from jax import lax
from jax.experimental import pallas as pl
from jax.experimental.pallas import tpu as pltpu
from jax.sharding import PartitionSpec as P

NX = 64
NY = 64
NZ = 64
CELLS = NX * NY * NZ
SCREENING = 0.01
PARTS = 16
PLANES = NX // PARTS
HALF = NY // 2
ROWS = HALF * PLANES
LANES = 128
STRIDE = 20


def turn(angles, sign):
    cosines, sines = np.cos(angles), sign * np.sin(angles)
    return np.array([[cosines, -sines], [sines, cosines]])


def tables():
    half, full = np.arange(HALF), np.arange(NY)
    two = np.arange(2)
    eye_x = np.eye(PLANES)
    order = np.array([2 * d + kl for kl in range(2) for d in range(PARTS)])
    rows = turn(2 * math.pi * (np.outer(order, half) % HALF) / HALF, -1)
    first = np.einsum("dckn,yx->dykcnx", rows, eye_x).reshape(2 * ROWS, 2 * ROWS)
    angles = 2 * math.pi / NY * order[None, :, None, None] * two[None, None, :, None]
    angles = np.broadcast_to(angles, (PLANES, HALF, 2, NZ)).reshape(ROWS, LANES)
    twiddle = np.stack([np.cos(angles), np.sin(angles)])
    depth = turn(2 * math.pi * (np.outer(full, full) % NZ) / NZ, -1)
    signs = np.array([[1.0, 1.0], [1.0, -1.0]])
    second = np.einsum("dckz,hb->cbzdhk", depth, signs).reshape(2 * LANES, 2 * LANES)
    term = 2.0 - 2.0 * np.cos(2 * math.pi * full / 64)
    excess = term[:, None] + term[None, :] + SCREENING
    kappa = 2.0 * np.arcsinh(0.5 * np.sqrt(excess))
    kappa = kappa.reshape(2, HALF, NZ).transpose(1, 0, 2).reshape(HALF, LANES)
    green = 1.0 / (2.0 * np.sinh(kappa)) / (NY * NZ)
    green[0, 0] = 0.0
    decay = np.stack([np.exp(-kappa * n)[order] for n in (1, 2, 3)])
    step = np.exp(-PLANES * kappa)
    close = 1.0 / (1.0 - np.exp(-NX * kappa))
    near = green * np.exp(-kappa)
    parts = np.stack([step, close, near]).reshape(3, PARTS, 1, 2, LANES)
    parts = np.broadcast_to(parts, (3, PARTS, 4, 2, LANES)).transpose(1, 0, 2, 3, 4).reshape(PARTS, 3, 8, LANES)
    line = np.array([0.0] + [1.0 / (t + SCREENING) for t in term[1:]])
    along = np.cos(2 * math.pi * (np.outer(full, full) % NX) / NX) @ line / NX / (NY * NZ)
    lag = along[(full[:, None] - full[None, :]) % NX]
    uniform = np.zeros((PARTS, 8, NX))
    uniform[:, :PLANES] = lag.reshape(PARTS, PLANES, NX)
    back = turn(2 * math.pi * (np.outer(full, full) % NZ) / NZ, 1)
    third = np.einsum("dczk,hb->chkdbz", back, signs).reshape(2 * LANES, 2 * LANES)
    columns = turn(2 * math.pi * (np.outer(half, order) % HALF) / HALF, 1)
    fourth = np.einsum("dcnk,yx->dyncxk", columns, eye_x).reshape(2 * ROWS, 2 * ROWS)
    names = ("first", "twiddle", "second", "green", "decay", "parts", "uniform", "third", "fourth")
    values = (first, twiddle, second, green[order], decay, parts, uniform, third, fourth)
    return {n: np.ascontiguousarray(v, dtype=np.float32) for n, v in zip(names, values)}


def dot(a, b):
    return jnp.dot(a, b, precision=lax.Precision.HIGHEST, preferred_element_type=jnp.float32)


def halves(values):
    top = values.astype(jnp.bfloat16)
    return top, (values - top.astype(jnp.float32)).astype(jnp.bfloat16)


def dot_halves(a, b):
    def product(x, y):
        return jnp.dot(x, y, preferred_element_type=jnp.float32)

    return product(a[0], b[0]) + (product(a[0], b[1]) + product(a[1], b[0]))


def density_spectra(electrons, holes, first, twiddle, second):
    real = jnp.zeros((ROWS, LANES), jnp.float32)
    imag = jnp.zeros((ROWS, LANES), jnp.float32)
    for band in range(electrons.shape[0]):
        e_re = electrons[band, 0].astype(jnp.float32)
        e_im = electrons[band, 1].astype(jnp.float32)
        h_re = holes[band, 0].astype(jnp.float32)
        h_im = holes[band, 1].astype(jnp.float32)
        real += e_re * h_re + e_im * h_im
        imag += e_re * h_im - e_im * h_re
    mixed = dot(first[...], jnp.concatenate([real, imag], axis=0))
    u_re, u_im = mixed[:ROWS], mixed[ROWS:]
    t_re = u_re * twiddle[0] + u_im * twiddle[1]
    t_im = u_im * twiddle[0] - u_re * twiddle[1]
    return dot(jnp.concatenate([t_re, t_im], axis=1), second[...])


def planes_of(spectra, c):
    return [spectra[x * HALF : (x + 1) * HALF, c * LANES : (c + 1) * LANES] for x in range(PLANES)]


def moments(spectra, decay):
    found = [[None, None], [None, None]]
    for c in range(2):
        planes = planes_of(spectra, c)
        for way, run in enumerate((planes, planes[::-1])):
            total = run[0]
            for plane in run[1:]:
                total = total * decay + plane
            found[way][c] = total
    return found


def own_kernel(rank, order, *refs):
    sources, (spectra, sums, mask, part, line) = refs[:8], refs[8:13]
    copies, sems = refs[13:19], refs[19]
    me = rank[0]
    sources = sources[:6] + (sources[6].at[me], sources[7].at[me])
    moves = [
        pltpu.make_async_copy(source, target, sems.at[n])
        for n, (source, target) in enumerate(zip(sources, copies + (part, line)))
    ]
    for move in moves:
        move.start()
    mask[...] = jnp.full((8, LANES), order[0, 0], jnp.int32)
    for move in moves:
        move.wait()
    electrons, holes, first, second, twiddle, decay = copies
    values = density_spectra(electrons, holes, first, twiddle, second)
    spectra[...] = values
    found = moments(values, decay[0])
    for way in range(2):
        for c in range(2):
            sums[way * 2 + c] = found[way][c]


def hold_kernel(*refs):
    for source, target in zip(refs[: len(refs) // 2], refs[len(refs) // 2 :]):
        target[...] = source[...]


def straight_of(mask, rows):
    return jnp.broadcast_to(mask[0:1], (rows, LANES)) == 0


def far_kernel(mask, electrons, holes, own, first, twiddle, second, decay, spectra, out):
    values = density_spectra(electrons, holes, first, twiddle, second)
    spectra[...] = values
    found = moments(values, decay[0])
    straight = straight_of(mask, HALF)
    for way in range(2):
        for c in range(2):
            near, far = own[way * 2 + c], found[way][c]
            pair = (jnp.where(straight, near, far), jnp.where(straight, far, near))
            for p in range(2):
                for kl in range(2):
                    row = way * 8 + p * 4 + c * 2 + kl
                    out[pl.ds(row, PARTS, stride=16), :] = pair[p][kl * PARTS : (kl + 1) * PARTS]


def total(values):
    return jnp.sum(values, axis=0, keepdims=True)


def local_terms(mask, own, far, green, decay, local):
    straight = straight_of(mask, HALF)
    weight = [green[...]] + [green[...] * decay[n] for n in range(3)]
    own_values, far_values = own[...], far[...]
    density, field = {}, {}
    for c in range(2):
        near, distant = planes_of(own_values, c), planes_of(far_values, c)
        for x in range(PLANES):
            density[0, c, x] = jnp.where(straight, near[x], distant[x])
            density[1, c, x] = jnp.where(straight, distant[x], near[x])
    for p in range(2):
        for c in range(2):
            for x in range(PLANES):
                value = weight[0] * density[p, c, x]
                for other in range(PLANES):
                    if other != x:
                        value += weight[abs(x - other)] * density[p, c, other]
                field[p, c, x] = value
                local[p, x * HALF : (x + 1) * HALF, c * LANES : (c + 1) * LANES] = value
    zero = jnp.zeros((HALF, LANES), jnp.float32)
    terms = [zero, zero, zero, zero]
    for x in range(PLANES):
        for c in range(2):
            terms[0] += field[0, c, x] * density[0, c, x]
            terms[1] += field[1, c, x] * density[1, c, x]
            terms[2] += field[0, c, x] * density[1, c, x]
        terms[3] += field[0, 1, x] * density[1, 0, x] - field[0, 0, x] * density[1, 1, x]
    lane = lax.broadcasted_iota(jnp.int32, (1, LANES), 1)
    rows = []
    for x in range(PLANES):
        row = jnp.zeros((1, LANES), jnp.float32)
        for p in range(2):
            for c in range(2):
                value = jnp.broadcast_to(density[p, c, x][0:1, 0:1], (1, LANES))
                row = jnp.where(lane // 16 == p * 2 + c, value, row)
        rows.append(row)
    return jnp.concatenate(rows, axis=0), [total(t) for t in terms]


def screen_kernel(block, part, mask, own, far, green, decay, out, local):
    ends, inner = local_terms(mask, own, far, green, decay, local)
    step, close, near = part[0], part[1], part[2]
    right = [block[s, 0:8] for s in range(PARTS)]
    left = [block[s, 8:16] for s in range(PARTS)]
    from_right, from_left = right[0], left[PARTS - 1]
    for n in range(1, PARTS):
        from_right = from_right * step + right[n]
        from_left = from_left * step + left[PARTS - 1 - n]
    from_right, from_left = from_right * close, from_left * close
    effect = {}
    for n in range(PARTS):
        effect[0, n] = near * from_right
        effect[1, PARTS - 1 - n] = near * from_left
        from_right = from_right * step + right[n]
        from_left = from_left * step + left[PARTS - 1 - n]
    zero = jnp.zeros((8, LANES), jnp.float32)
    same, cross, swapped = zero, zero, zero
    for s in range(PARTS):
        for way, moment in ((0, left[s]), (1, right[s])):
            value = effect[way, s]
            out[s * STRIDE + way * 8 : s * STRIDE + way * 8 + 8] = value
            turned = jnp.concatenate([moment[4:8], moment[0:4]], axis=0)
            same += value * moment
            cross += value * turned
            swapped += value * jnp.concatenate([moment[6:8], moment[4:6], moment[0:4]], axis=0)
    terms = [
        total(same[0:4]),
        total(same[4:8]),
        total(cross[0:4]),
        total(swapped[2:4]) - total(swapped[0:2]),
    ]
    terms = jnp.concatenate([a + b for a, b in zip(inner, terms)], axis=0)
    terms += pltpu.roll(terms, LANES // 2, 1)
    lane = lax.broadcasted_iota(jnp.int32, (PLANES, LANES), 1)
    ends = jnp.where(lane < LANES // 2, ends, terms)
    for s in range(PARTS):
        out[s * STRIDE + 16 : s * STRIDE + 20] = ends


def field_kernel(block, local, decay, twiddle, third, fourth, uniform, line, potential, coulomb):
    weight = [None, decay[0], decay[1], decay[2]]

    def effect(way, p, c):
        rows = [block[pl.ds(way * 8 + p * 4 + c * 2 + kl, PARTS, stride=STRIDE), :] for kl in range(2)]
        return jnp.concatenate(rows, axis=0)

    pairs = []
    for p in range(2):
        parts = []
        for c in range(2):
            right, left = effect(0, p, c), effect(1, p, c)
            planes = []
            for x in range(PLANES):
                value = local[p, x * HALF : (x + 1) * HALF, c * LANES : (c + 1) * LANES]
                value += right if x == 0 else right * weight[x]
                value += left if x == PLANES - 1 else left * weight[PLANES - 1 - x]
                planes.append(value)
            parts.append(jnp.concatenate(planes, axis=0))
        pairs.append(jnp.concatenate(parts, axis=1))
    mixed = dot_halves(halves(jnp.concatenate(pairs, axis=0)), (third[0], third[1]))
    columns = []
    for p in range(2):
        u_re, u_im = mixed[p * ROWS : (p + 1) * ROWS, :LANES], mixed[p * ROWS : (p + 1) * ROWS, LANES:]
        t_re = u_re * twiddle[0] - u_im * twiddle[1]
        t_im = u_im * twiddle[0] + u_re * twiddle[1]
        columns.append(jnp.concatenate([t_re, t_im], axis=0))
    ends = jnp.concatenate([block[STRIDE * s + 16 : STRIDE * s + 20] for s in range(PARTS)], axis=0)
    lane = lax.broadcasted_iota(jnp.int32, (NX, LANES), 1)
    plane = jnp.where(lane < LANES // 2, ends, 0.0)
    plane = plane - total(plane) * (1.0 / NX)
    own = dot(line[...], plane)
    lane = lax.broadcasted_iota(jnp.int32, (8, LANES), 1)
    shift = [
        jnp.where(
            lane < NZ,
            jnp.broadcast_to(own[:, 32 * p : 32 * p + 1], (8, LANES)),
            jnp.broadcast_to(own[:, 32 * p + 16 : 32 * p + 17], (8, LANES)),
        )
        for p in range(2)
    ]
    lane = lax.broadcasted_iota(jnp.int32, (HALF, LANES), 1)
    values = dot_halves((fourth[0], fourth[1]), halves(jnp.concatenate(columns, axis=1)))
    for p in range(2):
        for x in range(PLANES):
            re = values[x * HALF : (x + 1) * HALF, p * LANES : (p + 1) * LANES]
            im = values[ROWS + x * HALF : ROWS + (x + 1) * HALF, p * LANES : (p + 1) * LANES]
            even = jnp.where(lane < NZ, re, pltpu.roll(im, NZ, 1))
            odd = jnp.where(lane < NZ, pltpu.roll(re, NZ, 1), im)
            potential[p, x, pl.ds(0, HALF, stride=2), :] = even + shift[p][x : x + 1]
            potential[p, x, pl.ds(1, HALF, stride=2), :] = odd + shift[p][x : x + 1]
    line_all = jnp.concatenate([uniform[s, 0:PLANES] for s in range(PARTS)], axis=0)
    level = dot(line_all, plane)
    lane = lax.broadcasted_iota(jnp.int32, (1, LANES), 1)
    same = total(level * plane) * (1.0 / 16)
    cross = total(level * pltpu.roll(plane, 96, 1)) * (1.0 / 16)
    swapped = total(jnp.where(lane < 16, -level * pltpu.roll(plane, 80, 1), level * pltpu.roll(plane, 112, 1))) * (1.0 / 16)
    ahead = lane < 32
    extra = [jnp.where(ahead, same, 0.0), jnp.where(ahead, 0.0, same), jnp.where(ahead, cross, 0.0), jnp.where(ahead, swapped, 0.0)]
    sums = ends[0:PLANES]
    for s in range(1, PARTS):
        sums += ends[s * PLANES : (s + 1) * PLANES]
    sums = jnp.where(lane < LANES // 2, 0.0, sums) + jnp.concatenate(extra, axis=0)
    sums = jnp.sum(sums, axis=1, keepdims=True) * (1.0 / CELLS)
    c00, c11, re, im = (sums[k : k + 1] for k in range(4))
    row = lax.broadcasted_iota(jnp.int32, (2, 2), 0)
    col = lax.broadcasted_iota(jnp.int32, (2, 2), 1)
    coulomb[0] = jnp.where(row == col, jnp.where(row == 0, c00, c11), re)
    coulomb[1] = jnp.where(row == col, 0.0, jnp.where(row == 0, im, -im))


def full(memory_space=pltpu.VMEM):
    return pl.BlockSpec(memory_space=memory_space)


def call(kernel, name, out_shape, *operands, scalars=0, space=pltpu.VMEM, scratch=(), limit=32):
    specs = [full(pltpu.SMEM)] * scalars + [full(space)] * (len(operands) - scalars)
    several = isinstance(out_shape, (list, tuple))
    return pl.pallas_call(
        kernel,
        out_shape=out_shape,
        in_specs=specs,
        out_specs=[full()] * len(out_shape) if several else full(),
        scratch_shapes=scratch,
        compiler_params=pltpu.CompilerParams(vmem_limit_bytes=limit * 1024 * 1024),
        name=name,
    )(*operands)


def shape(*dims, dtype=jnp.float32):
    return jax.ShapeDtypeStruct(dims, dtype)


def tiled_states(states):
    bands = states.shape[1]
    parts = states.reshape(bands, 2, PLANES, HALF, LANES)
    return parts.transpose(0, 1, 3, 2, 4).reshape(bands, 2, ROWS, LANES)


def split_table(values):
    top = values.astype(ml_dtypes.bfloat16)
    rest = (values - top.astype(np.float32)).astype(ml_dtypes.bfloat16)
    return jnp.asarray(np.stack([top, rest]))


def shards(electrons, holes, pair_order):
    found = tables()
    t = {name: jnp.asarray(value) for name, value in found.items()}
    third, fourth = split_table(found["third"]), split_table(found["fourth"])
    groups = lax.axis_size("blk")
    rank = lax.axis_index("space").astype(jnp.int32).reshape(1)
    previous = lax.ppermute(holes, "blk", [((i - 1) % groups, i) for i in range(groups)])
    e = tiled_states(electrons)
    spectra = shape(ROWS, 2 * LANES)
    h = tiled_states(holes)
    brought = (e, h, t["first"], t["second"], t["twiddle"], t["decay"])
    made = call(
        own_kernel, "own_pair",
        [spectra, shape(4, HALF, LANES), shape(8, LANES, dtype=jnp.int32), shape(3, 8, LANES), shape(8, NX)],
        rank, pair_order, *brought, t["parts"], t["uniform"],
        scalars=2, space=pltpu.HBM, limit=60,
        scratch=[pltpu.VMEM(x.shape, x.dtype) for x in brought] + [pltpu.SemaphoreType.DMA((8,))],
    )
    own, sums, mask, part, line = call(
        hold_kernel, "hold", [jax.ShapeDtypeStruct(x.shape, x.dtype) for x in made], *made
    )
    far, sent = call(
        far_kernel, "far_pair", [spectra, shape(PARTS * 16, LANES)],
        mask, e, tiled_states(previous), sums, t["first"], t["twiddle"], t["second"], t["decay"],
    )
    blocks = lax.all_to_all(sent.reshape(PARTS, 16, LANES), "space", split_axis=0, concat_axis=0, tiled=True)
    effects, local = call(
        screen_kernel, "screen", [shape(PARTS * STRIDE, LANES), shape(2, ROWS, 2 * LANES)],
        blocks, part, mask, own, far, t["green"], t["decay"],
    )
    effects = effects.reshape(PARTS, STRIDE // 4, 4, LANES)
    effects = lax.all_to_all(effects, "space", split_axis=0, concat_axis=0, tiled=True)
    potential, coulomb = call(
        field_kernel, "field", [shape(2, PLANES, NY, LANES), shape(2, 2, 2)],
        effects.reshape(PARTS * STRIDE, LANES), local, t["decay"], t["twiddle"], third, fourth, t["uniform"], line,
    )
    return (potential[None], coulomb[None])


def solution(mesh):
    in_specs = (
        P("blk", None, None, "space", None),
        P("blk", None, None, "space", None),
        P("blk", None),
    )
    out_specs = (P("blk", None, "space", None, None), P("blk", None, None, None))
    return jax.shard_map(shards, mesh=mesh, in_specs=in_specs, out_specs=out_specs, check_vma=False)
```

```python
import math

import jax
import jax.numpy as jnp
import ml_dtypes
import numpy as np
from jax import lax
from jax.experimental import pallas as pl
from jax.experimental.pallas import tpu as pltpu
from jax.sharding import PartitionSpec as P

NX = 64
NY = 64
NZ = 64
CELLS = NX * NY * NZ
SCREENING = 0.01
PARTS = 16
PLANES = NX // PARTS
HALF = NY // 2
ROWS = HALF * PLANES
LANES = 128
STRIDE = 20


def turn(angles, sign):
    cosines, sines = np.cos(angles), sign * np.sin(angles)
    return np.array([[cosines, -sines], [sines, cosines]])


def tables():
    half, full = np.arange(HALF), np.arange(NY)
    two = np.arange(2)
    eye_x = np.eye(PLANES)
    order = np.array([2 * d + kl for kl in range(2) for d in range(PARTS)])
    rows = turn(2 * math.pi * (np.outer(order, half) % HALF) / HALF, -1)
    first = np.einsum("dckn,yx->dykcnx", rows, eye_x).reshape(2 * ROWS, 2 * ROWS)
    angles = 2 * math.pi / NY * order[None, :, None, None] * two[None, None, :, None]
    angles = np.broadcast_to(angles, (PLANES, HALF, 2, NZ)).reshape(ROWS, LANES)
    twiddle = np.stack([np.cos(angles), np.sin(angles)])
    depth = turn(2 * math.pi * (np.outer(full, full) % NZ) / NZ, -1)
    signs = np.array([[1.0, 1.0], [1.0, -1.0]])
    second = np.einsum("dckz,hb->cbzdhk", depth, signs).reshape(2 * LANES, 2 * LANES)
    term = 2.0 - 2.0 * np.cos(2 * math.pi * full / 64)
    excess = term[:, None] + term[None, :] + SCREENING
    kappa = 2.0 * np.arcsinh(0.5 * np.sqrt(excess))
    kappa = kappa.reshape(2, HALF, NZ).transpose(1, 0, 2).reshape(HALF, LANES)
    green = 1.0 / (2.0 * np.sinh(kappa)) / (NY * NZ)
    green[0, 0] = 0.0
    decay = np.stack([np.exp(-kappa * n)[order] for n in (1, 2, 3)])
    step = np.exp(-PLANES * kappa)
    close = 1.0 / (1.0 - np.exp(-NX * kappa))
    near = green * np.exp(-kappa)
    parts = np.stack([step, close, near]).reshape(3, PARTS, 1, 2, LANES)
    parts = np.broadcast_to(parts, (3, PARTS, 4, 2, LANES)).transpose(1, 0, 2, 3, 4).reshape(PARTS, 3, 8, LANES)
    line = np.array([0.0] + [1.0 / (t + SCREENING) for t in term[1:]])
    along = np.cos(2 * math.pi * (np.outer(full, full) % NX) / NX) @ line / NX / (NY * NZ)
    lag = along[(full[:, None] - full[None, :]) % NX]
    uniform = np.zeros((PARTS, 8, NX))
    uniform[:, :PLANES] = lag.reshape(PARTS, PLANES, NX)
    back = turn(2 * math.pi * (np.outer(full, full) % NZ) / NZ, 1)
    third = np.einsum("dczk,hb->chkdbz", back, signs).reshape(2 * LANES, 2 * LANES)
    columns = turn(2 * math.pi * (np.outer(half, order) % HALF) / HALF, 1)
    fourth = np.einsum("dcnk,yx->dyncxk", columns, eye_x).reshape(2 * ROWS, 2 * ROWS)
    names = ("first", "twiddle", "second", "green", "decay", "parts", "uniform", "third", "fourth")
    values = (first, twiddle, second, green[order], decay, parts, uniform, third, fourth)
    return {n: np.ascontiguousarray(v, dtype=np.float32) for n, v in zip(names, values)}


def dot(a, b):
    return jnp.dot(a, b, precision=lax.Precision.HIGHEST, preferred_element_type=jnp.float32)


def halves(values):
    top = values.astype(jnp.bfloat16)
    return top, (values - top.astype(jnp.float32)).astype(jnp.bfloat16)


def dot_halves(a, b):
    def product(x, y):
        return jnp.dot(x, y, preferred_element_type=jnp.float32)

    return product(a[0], b[0]) + (product(a[0], b[1]) + product(a[1], b[0]))


def left_halves(table, values):
    parts = halves(values)
    width = values.shape[1]
    both = jnp.dot(table[0], jnp.concatenate(parts, axis=1), preferred_element_type=jnp.float32)
    rest = jnp.dot(table[1], parts[0], preferred_element_type=jnp.float32)
    return both[:, :width] + (both[:, width:] + rest)


def right_halves(values, table):
    parts = halves(values)
    height = values.shape[0]
    both = jnp.dot(jnp.concatenate(parts, axis=0), table[0], preferred_element_type=jnp.float32)
    rest = jnp.dot(parts[0], table[1], preferred_element_type=jnp.float32)
    return both[:height] + (both[height:] + rest)


def with_first_row(values, rows):
    first = lax.broadcasted_iota(jnp.int32, (8, values.shape[1]), 0) == 0
    pieces = []
    for x in range(PLANES):
        own = values[x * HALF : (x + 1) * HALF]
        pieces += [jnp.where(first, rows[x : x + 1], own[:8]), own[8:]]
    return jnp.concatenate(pieces, axis=0)


def density_spectra(electrons, holes, first, twiddle, second):
    real = jnp.zeros((ROWS, LANES), jnp.float32)
    imag = jnp.zeros((ROWS, LANES), jnp.float32)
    for band in range(electrons.shape[0]):
        e_re = electrons[band, 0].astype(jnp.float32)
        e_im = electrons[band, 1].astype(jnp.float32)
        h_re = holes[band, 0].astype(jnp.float32)
        h_im = holes[band, 1].astype(jnp.float32)
        real += e_re * h_re + e_im * h_im
        imag += e_re * h_im - e_im * h_re
    around, column, level = [], [], []
    for part in (real, imag):
        rows = part[0:8]
        for k in range(1, ROWS // 8):
            rows = rows + part[k * 8 : k * 8 + 8]
        mean = (rows[0:4] + rows[4:8]) * (1.0 / HALF)
        grand = jnp.sum(mean, axis=1, keepdims=True) * (1.0 / LANES)
        around.append(part - jnp.concatenate([mean] * HALF, axis=0))
        column.append((mean - grand) * HALF)
        level.append(grand * (NY * NZ))
    mixed = left_halves(first, jnp.concatenate(around, axis=0))
    u_re, u_im = mixed[:ROWS], mixed[ROWS:]
    t_re = with_first_row(u_re * twiddle[0] + u_im * twiddle[1], column[0])
    t_im = with_first_row(u_im * twiddle[0] - u_re * twiddle[1], column[1])
    values = right_halves(jnp.concatenate([t_re, t_im], axis=1), second)
    lane = lax.broadcasted_iota(jnp.int32, (PLANES, LANES), 1)
    parts = []
    for c in range(2):
        part = values[:, c * LANES : (c + 1) * LANES]
        rows = jnp.concatenate([part[x * HALF : x * HALF + 1] for x in range(PLANES)], axis=0)
        parts.append(with_first_row(part, rows + jnp.where(lane == 0, level[c], 0.0)))
    return jnp.concatenate(parts, axis=1)


def planes_of(spectra, c):
    return [spectra[x * HALF : (x + 1) * HALF, c * LANES : (c + 1) * LANES] for x in range(PLANES)]


def moments(spectra, decay):
    found = [[None, None], [None, None]]
    for c in range(2):
        planes = planes_of(spectra, c)
        for way, run in enumerate((planes, planes[::-1])):
            total = run[0]
            for plane in run[1:]:
                total = total * decay + plane
            found[way][c] = total
    return found


def own_kernel(rank, order, *refs):
    sources, (spectra, sums, mask, part, line) = refs[:8], refs[8:13]
    copies, sems = refs[13:19], refs[19]
    me = rank[0]
    sources = sources[:6] + (sources[6].at[me], sources[7].at[me])
    moves = [
        pltpu.make_async_copy(source, target, sems.at[n])
        for n, (source, target) in enumerate(zip(sources, copies + (part, line)))
    ]
    for move in moves:
        move.start()
    mask[...] = jnp.full((8, LANES), order[0, 0], jnp.int32)
    for move in moves:
        move.wait()
    electrons, holes, first, second, twiddle, decay = copies
    values = density_spectra(electrons, holes, first, twiddle, second)
    spectra[...] = values
    found = moments(values, decay[0])
    for way in range(2):
        for c in range(2):
            sums[way * 2 + c] = found[way][c]


def hold_kernel(*refs):
    for source, target in zip(refs[: len(refs) // 2], refs[len(refs) // 2 :]):
        target[...] = source[...]


def straight_of(mask, rows):
    return jnp.broadcast_to(mask[0:1], (rows, LANES)) == 0


def far_kernel(mask, electrons, holes, own, first, twiddle, second, decay, spectra, out):
    values = density_spectra(electrons, holes, first, twiddle, second)
    spectra[...] = values
    found = moments(values, decay[0])
    straight = straight_of(mask, HALF)
    for way in range(2):
        for c in range(2):
            near, far = own[way * 2 + c], found[way][c]
            pair = (jnp.where(straight, near, far), jnp.where(straight, far, near))
            for p in range(2):
                for kl in range(2):
                    row = way * 8 + p * 4 + c * 2 + kl
                    out[pl.ds(row, PARTS, stride=16), :] = pair[p][kl * PARTS : (kl + 1) * PARTS]


def total(values):
    return jnp.sum(values, axis=0, keepdims=True)


def local_terms(mask, own, far, green, decay, local):
    straight = straight_of(mask, HALF)
    weight = [green[...]] + [green[...] * decay[n] for n in range(3)]
    own_values, far_values = own[...], far[...]
    density, field = {}, {}
    for c in range(2):
        near, distant = planes_of(own_values, c), planes_of(far_values, c)
        for x in range(PLANES):
            density[0, c, x] = jnp.where(straight, near[x], distant[x])
            density[1, c, x] = jnp.where(straight, distant[x], near[x])
    for p in range(2):
        for c in range(2):
            for x in range(PLANES):
                value = weight[0] * density[p, c, x]
                for other in range(PLANES):
                    if other != x:
                        value += weight[abs(x - other)] * density[p, c, other]
                field[p, c, x] = value
                local[p, x * HALF : (x + 1) * HALF, c * LANES : (c + 1) * LANES] = value
    zero = jnp.zeros((HALF, LANES), jnp.float32)
    terms = [zero, zero, zero, zero]
    for x in range(PLANES):
        for c in range(2):
            terms[0] += field[0, c, x] * density[0, c, x]
            terms[1] += field[1, c, x] * density[1, c, x]
            terms[2] += field[0, c, x] * density[1, c, x]
        terms[3] += field[0, 1, x] * density[1, 0, x] - field[0, 0, x] * density[1, 1, x]
    lane = lax.broadcasted_iota(jnp.int32, (1, LANES), 1)
    rows = []
    for x in range(PLANES):
        row = jnp.zeros((1, LANES), jnp.float32)
        for p in range(2):
            for c in range(2):
                value = jnp.broadcast_to(density[p, c, x][0:1, 0:1], (1, LANES))
                row = jnp.where(lane // 16 == p * 2 + c, value, row)
        rows.append(row)
    return jnp.concatenate(rows, axis=0), [total(t) for t in terms]


def screen_kernel(block, part, mask, own, far, green, decay, out, local):
    ends, inner = local_terms(mask, own, far, green, decay, local)
    step, close, near = part[0], part[1], part[2]
    right = [block[s, 0:8] for s in range(PARTS)]
    left = [block[s, 8:16] for s in range(PARTS)]
    from_right, from_left = right[0], left[PARTS - 1]
    for n in range(1, PARTS):
        from_right = from_right * step + right[n]
        from_left = from_left * step + left[PARTS - 1 - n]
    from_right, from_left = from_right * close, from_left * close
    effect = {}
    for n in range(PARTS):
        effect[0, n] = near * from_right
        effect[1, PARTS - 1 - n] = near * from_left
        from_right = from_right * step + right[n]
        from_left = from_left * step + left[PARTS - 1 - n]
    zero = jnp.zeros((8, LANES), jnp.float32)
    same, cross, swapped = zero, zero, zero
    for s in range(PARTS):
        for way, moment in ((0, left[s]), (1, right[s])):
            value = effect[way, s]
            out[s * STRIDE + way * 8 : s * STRIDE + way * 8 + 8] = value
            turned = jnp.concatenate([moment[4:8], moment[0:4]], axis=0)
            same += value * moment
            cross += value * turned
            swapped += value * jnp.concatenate([moment[6:8], moment[4:6], moment[0:4]], axis=0)
    terms = [
        total(same[0:4]),
        total(same[4:8]),
        total(cross[0:4]),
        total(swapped[2:4]) - total(swapped[0:2]),
    ]
    terms = jnp.concatenate([a + b for a, b in zip(inner, terms)], axis=0)
    terms += pltpu.roll(terms, LANES // 2, 1)
    lane = lax.broadcasted_iota(jnp.int32, (PLANES, LANES), 1)
    ends = jnp.where(lane < LANES // 2, ends, terms)
    for s in range(PARTS):
        out[s * STRIDE + 16 : s * STRIDE + 20] = ends


def field_kernel(block, local, decay, twiddle, third, fourth, uniform, line, potential, coulomb):
    weight = [None, decay[0], decay[1], decay[2]]

    def effect(way, p, c):
        rows = [block[pl.ds(way * 8 + p * 4 + c * 2 + kl, PARTS, stride=STRIDE), :] for kl in range(2)]
        return jnp.concatenate(rows, axis=0)

    pairs = []
    for p in range(2):
        parts = []
        for c in range(2):
            right, left = effect(0, p, c), effect(1, p, c)
            planes = []
            for x in range(PLANES):
                value = local[p, x * HALF : (x + 1) * HALF, c * LANES : (c + 1) * LANES]
                value += right if x == 0 else right * weight[x]
                value += left if x == PLANES - 1 else left * weight[PLANES - 1 - x]
                planes.append(value)
            parts.append(jnp.concatenate(planes, axis=0))
        pairs.append(jnp.concatenate(parts, axis=1))
    mixed = dot_halves(halves(jnp.concatenate(pairs, axis=0)), (third[0], third[1]))
    columns = []
    for p in range(2):
        u_re, u_im = mixed[p * ROWS : (p + 1) * ROWS, :LANES], mixed[p * ROWS : (p + 1) * ROWS, LANES:]
        t_re = u_re * twiddle[0] - u_im * twiddle[1]
        t_im = u_im * twiddle[0] + u_re * twiddle[1]
        columns.append(jnp.concatenate([t_re, t_im], axis=0))
    ends = jnp.concatenate([block[STRIDE * s + 16 : STRIDE * s + 20] for s in range(PARTS)], axis=0)
    lane = lax.broadcasted_iota(jnp.int32, (NX, LANES), 1)
    plane = jnp.where(lane < LANES // 2, ends, 0.0)
    plane = plane - total(plane) * (1.0 / NX)
    own = dot(line[...], plane)
    lane = lax.broadcasted_iota(jnp.int32, (8, LANES), 1)
    shift = [
        jnp.where(
            lane < NZ,
            jnp.broadcast_to(own[:, 32 * p : 32 * p + 1], (8, LANES)),
            jnp.broadcast_to(own[:, 32 * p + 16 : 32 * p + 17], (8, LANES)),
        )
        for p in range(2)
    ]
    lane = lax.broadcasted_iota(jnp.int32, (HALF, LANES), 1)
    values = dot_halves((fourth[0], fourth[1]), halves(jnp.concatenate(columns, axis=1)))
    for p in range(2):
        for x in range(PLANES):
            re = values[x * HALF : (x + 1) * HALF, p * LANES : (p + 1) * LANES]
            im = values[ROWS + x * HALF : ROWS + (x + 1) * HALF, p * LANES : (p + 1) * LANES]
            even = jnp.where(lane < NZ, re, pltpu.roll(im, NZ, 1))
            odd = jnp.where(lane < NZ, pltpu.roll(re, NZ, 1), im)
            potential[p, x, pl.ds(0, HALF, stride=2), :] = even + shift[p][x : x + 1]
            potential[p, x, pl.ds(1, HALF, stride=2), :] = odd + shift[p][x : x + 1]
    line_all = jnp.concatenate([uniform[s, 0:PLANES] for s in range(PARTS)], axis=0)
    level = dot(line_all, plane)
    lane = lax.broadcasted_iota(jnp.int32, (1, LANES), 1)
    same = total(level * plane) * (1.0 / 16)
    cross = total(level * pltpu.roll(plane, 96, 1)) * (1.0 / 16)
    swapped = total(jnp.where(lane < 16, -level * pltpu.roll(plane, 80, 1), level * pltpu.roll(plane, 112, 1))) * (1.0 / 16)
    ahead = lane < 32
    extra = [jnp.where(ahead, same, 0.0), jnp.where(ahead, 0.0, same), jnp.where(ahead, cross, 0.0), jnp.where(ahead, swapped, 0.0)]
    sums = ends[0:PLANES]
    for s in range(1, PARTS):
        sums += ends[s * PLANES : (s + 1) * PLANES]
    sums = jnp.where(lane < LANES // 2, 0.0, sums) + jnp.concatenate(extra, axis=0)
    sums = jnp.sum(sums, axis=1, keepdims=True) * (1.0 / CELLS)
    c00, c11, re, im = (sums[k : k + 1] for k in range(4))
    row = lax.broadcasted_iota(jnp.int32, (2, 2), 0)
    col = lax.broadcasted_iota(jnp.int32, (2, 2), 1)
    coulomb[0] = jnp.where(row == col, jnp.where(row == 0, c00, c11), re)
    coulomb[1] = jnp.where(row == col, 0.0, jnp.where(row == 0, im, -im))


def full(memory_space=pltpu.VMEM):
    return pl.BlockSpec(memory_space=memory_space)


def call(kernel, name, out_shape, *operands, scalars=0, space=pltpu.VMEM, scratch=(), limit=32):
    specs = [full(pltpu.SMEM)] * scalars + [full(space)] * (len(operands) - scalars)
    several = isinstance(out_shape, (list, tuple))
    return pl.pallas_call(
        kernel,
        out_shape=out_shape,
        in_specs=specs,
        out_specs=[full()] * len(out_shape) if several else full(),
        scratch_shapes=scratch,
        compiler_params=pltpu.CompilerParams(vmem_limit_bytes=limit * 1024 * 1024),
        name=name,
    )(*operands)


def shape(*dims, dtype=jnp.float32):
    return jax.ShapeDtypeStruct(dims, dtype)


def tiled_states(states):
    bands = states.shape[1]
    parts = states.reshape(bands, 2, PLANES, HALF, LANES)
    return parts.transpose(0, 1, 3, 2, 4).reshape(bands, 2, ROWS, LANES)


def split_table(values):
    top = values.astype(ml_dtypes.bfloat16)
    rest = (values - top.astype(np.float32)).astype(ml_dtypes.bfloat16)
    return jnp.asarray(np.stack([top, rest]))


def shards(electrons, holes, pair_order):
    found = tables()
    t = {name: jnp.asarray(value) for name, value in found.items()}
    for name in ("first", "second", "third", "fourth"):
        t[name] = split_table(found[name])
    groups = lax.axis_size("blk")
    rank = lax.axis_index("space").astype(jnp.int32).reshape(1)
    previous = lax.ppermute(holes, "blk", [((i - 1) % groups, i) for i in range(groups)])
    e = tiled_states(electrons)
    spectra = shape(ROWS, 2 * LANES)
    h = tiled_states(holes)
    brought = (e, h, t["first"], t["second"], t["twiddle"], t["decay"])
    made = call(
        own_kernel, "own_pair",
        [spectra, shape(4, HALF, LANES), shape(8, LANES, dtype=jnp.int32), shape(3, 8, LANES), shape(8, NX)],
        rank, pair_order, *brought, t["parts"], t["uniform"],
        scalars=2, space=pltpu.HBM, limit=60,
        scratch=[pltpu.VMEM(x.shape, x.dtype) for x in brought] + [pltpu.SemaphoreType.DMA((8,))],
    )
    own, sums, mask, part, line = call(
        hold_kernel, "hold", [jax.ShapeDtypeStruct(x.shape, x.dtype) for x in made], *made
    )
    far, sent = call(
        far_kernel, "far_pair", [spectra, shape(PARTS * 16, LANES)],
        mask, e, tiled_states(previous), sums, t["first"], t["twiddle"], t["second"], t["decay"],
    )
    blocks = lax.all_to_all(sent.reshape(PARTS, 16, LANES), "space", split_axis=0, concat_axis=0, tiled=True)
    effects, local = call(
        screen_kernel, "screen", [shape(PARTS * STRIDE, LANES), shape(2, ROWS, 2 * LANES)],
        blocks, part, mask, own, far, t["green"], t["decay"],
    )
    effects = effects.reshape(PARTS, STRIDE // 4, 4, LANES)
    effects = lax.all_to_all(effects, "space", split_axis=0, concat_axis=0, tiled=True)
    potential, coulomb = call(
        field_kernel, "field", [shape(2, PLANES, NY, LANES), shape(2, 2, 2)],
        effects.reshape(PARTS * STRIDE, LANES), local, t["decay"], t["twiddle"], t["third"], t["fourth"], t["uniform"], line,
    )
    return (potential[None], coulomb[None])


def solution(mesh):
    in_specs = (
        P("blk", None, None, "space", None),
        P("blk", None, None, "space", None),
        P("blk", None),
    )
    out_specs = (P("blk", None, "space", None, None), P("blk", None, None, None))
    return jax.shard_map(shards, mesh=mesh, in_specs=in_specs, out_specs=out_specs, check_vma=False)
```

```python
import math

import jax
import jax.numpy as jnp
import ml_dtypes
import numpy as np
from jax import lax
from jax.experimental import pallas as pl
from jax.experimental.pallas import tpu as pltpu
from jax.sharding import PartitionSpec as P

NX = 64
NY = 64
NZ = 64
CELLS = NX * NY * NZ
SCREENING = 0.01
PARTS = 16
PLANES = NX // PARTS
HALF = NY // 2
ROWS = HALF * PLANES
LANES = 128
SUMS, PART, LINE, MASK, PACKED = 256, 384, 408, 416, 424
STRIDE = 20


def turn(angles, sign):
    cosines, sines = np.cos(angles), sign * np.sin(angles)
    return np.array([[cosines, -sines], [sines, cosines]])


def tables():
    half, full = np.arange(HALF), np.arange(NY)
    two = np.arange(2)
    eye_x = np.eye(PLANES)
    order = np.array([2 * d + kl for kl in range(2) for d in range(PARTS)])
    rows = turn(2 * math.pi * (np.outer(order, half) % HALF) / HALF, -1)
    first = np.einsum("dckn,yx->dykcnx", rows, eye_x).reshape(2 * ROWS, 2 * ROWS)
    angles = 2 * math.pi / NY * order[None, :, None, None] * two[None, None, :, None]
    angles = np.broadcast_to(angles, (PLANES, HALF, 2, NZ)).reshape(ROWS, LANES)
    twiddle = np.stack([np.cos(angles), np.sin(angles)])
    depth = turn(2 * math.pi * (np.outer(full, full) % NZ) / NZ, -1)
    signs = np.array([[1.0, 1.0], [1.0, -1.0]])
    second = np.einsum("dckz,hb->cbzdhk", depth, signs).reshape(2 * LANES, 2 * LANES)
    term = 2.0 - 2.0 * np.cos(2 * math.pi * full / 64)
    excess = term[:, None] + term[None, :] + SCREENING
    kappa = 2.0 * np.arcsinh(0.5 * np.sqrt(excess))
    kappa = kappa.reshape(2, HALF, NZ).transpose(1, 0, 2).reshape(HALF, LANES)
    green = 1.0 / (2.0 * np.sinh(kappa)) / (NY * NZ)
    green[0, 0] = 0.0
    decay = np.stack([np.exp(-kappa * n)[order] for n in (1, 2, 3)])
    step = np.exp(-PLANES * kappa)
    close = 1.0 / (1.0 - np.exp(-NX * kappa))
    near = green * np.exp(-kappa)
    parts = np.stack([step, close, near]).reshape(3, PARTS, 1, 2, LANES)
    parts = np.broadcast_to(parts, (3, PARTS, 4, 2, LANES)).transpose(1, 0, 2, 3, 4).reshape(PARTS, 24, LANES)
    line = np.array([0.0] + [1.0 / (t + SCREENING) for t in term[1:]])
    along = np.cos(2 * math.pi * (np.outer(full, full) % NX) / NX) @ line / NX / (NY * NZ)
    lag = along[(full[:, None] - full[None, :]) % NX]
    uniform = np.zeros((PARTS, 8, LANES))
    uniform[:, :PLANES, :NX] = lag.reshape(PARTS, PLANES, NX)
    back = turn(2 * math.pi * (np.outer(full, full) % NZ) / NZ, 1)
    third = np.einsum("dczk,hb->chkdbz", back, signs).reshape(2 * LANES, 2 * LANES)
    columns = turn(2 * math.pi * (np.outer(half, order) % HALF) / HALF, 1)
    fourth = np.einsum("dcnk,yx->dyncxk", columns, eye_x).reshape(2 * ROWS, 2 * ROWS)
    names = ("first", "twiddle", "second", "green", "decay", "parts", "uniform", "third", "fourth")
    values = (first, twiddle, second, green[order], decay, parts, uniform, third, fourth)
    return {n: np.ascontiguousarray(v, dtype=np.float32) for n, v in zip(names, values)}


def dot(a, b):
    return jnp.dot(a, b, precision=lax.Precision.HIGHEST, preferred_element_type=jnp.float32)


def halves(values):
    top = values.astype(jnp.bfloat16)
    return top, (values - top.astype(jnp.float32)).astype(jnp.bfloat16)


def dot_halves(a, b):
    def product(x, y):
        return jnp.dot(x, y, preferred_element_type=jnp.float32)

    return product(a[0], b[0]) + (product(a[0], b[1]) + product(a[1], b[0]))


def left_halves(table, values):
    parts = halves(values)
    width = values.shape[1]
    both = jnp.dot(table[0], jnp.concatenate(parts, axis=1), preferred_element_type=jnp.float32)
    rest = jnp.dot(table[1], parts[0], preferred_element_type=jnp.float32)
    return both[:, :width] + (both[:, width:] + rest)


def right_halves(values, table):
    parts = halves(values)
    height = values.shape[0]
    both = jnp.dot(jnp.concatenate(parts, axis=0), table[0], preferred_element_type=jnp.float32)
    rest = jnp.dot(parts[0], table[1], preferred_element_type=jnp.float32)
    return both[:height] + (both[height:] + rest)


def with_first_row(values, rows):
    first = lax.broadcasted_iota(jnp.int32, (8, values.shape[1]), 0) == 0
    pieces = []
    for x in range(PLANES):
        own = values[x * HALF : (x + 1) * HALF]
        pieces += [jnp.where(first, rows[x : x + 1], own[:8]), own[8:]]
    return jnp.concatenate(pieces, axis=0)


def density_spectra(electrons, holes, first, twiddle, second):
    real = jnp.zeros((ROWS, LANES), jnp.float32)
    imag = jnp.zeros((ROWS, LANES), jnp.float32)
    for band in range(electrons.shape[0]):
        e_re = electrons[band, 0].astype(jnp.float32)
        e_im = electrons[band, 1].astype(jnp.float32)
        h_re = holes[band, 0].astype(jnp.float32)
        h_im = holes[band, 1].astype(jnp.float32)
        real += e_re * h_re + e_im * h_im
        imag += e_re * h_im - e_im * h_re
    around, column, level = [], [], []
    for part in (real, imag):
        rows = part[0:8]
        for k in range(1, ROWS // 8):
            rows = rows + part[k * 8 : k * 8 + 8]
        mean = (rows[0:4] + rows[4:8]) * (1.0 / HALF)
        grand = jnp.sum(mean, axis=1, keepdims=True) * (1.0 / LANES)
        around.append(part - jnp.concatenate([mean] * HALF, axis=0))
        column.append((mean - grand) * HALF)
        level.append(grand * (NY * NZ))
    mixed = left_halves(first, jnp.concatenate(around, axis=0))
    u_re, u_im = mixed[:ROWS], mixed[ROWS:]
    t_re = with_first_row(u_re * twiddle[0] + u_im * twiddle[1], column[0])
    t_im = with_first_row(u_im * twiddle[0] - u_re * twiddle[1], column[1])
    values = right_halves(jnp.concatenate([t_re, t_im], axis=1), second)
    lane = lax.broadcasted_iota(jnp.int32, (PLANES, LANES), 1)
    parts = []
    for c in range(2):
        part = values[:, c * LANES : (c + 1) * LANES]
        rows = jnp.concatenate([part[x * HALF : x * HALF + 1] for x in range(PLANES)], axis=0)
        parts.append(with_first_row(part, rows + jnp.where(lane == 0, level[c], 0.0)))
    return jnp.concatenate(parts, axis=1)


def planes_of(spectra, c):
    return [spectra[x * HALF : (x + 1) * HALF, c * LANES : (c + 1) * LANES] for x in range(PLANES)]


def moments(spectra, decay):
    found = [[None, None], [None, None]]
    for c in range(2):
        planes = planes_of(spectra, c)
        for way, run in enumerate((planes, planes[::-1])):
            total = run[0]
            for plane in run[1:]:
                total = total * decay + plane
            found[way][c] = total
    return found


def own_kernel(rank, order, *refs):
    sources, pack, copies, sems = refs[:8], refs[8], refs[9:15], refs[15]
    me = rank[0]
    sources = sources[:6] + (sources[6].at[me], sources[7].at[me])
    targets = copies + (pack.at[PART : PART + 24], pack.at[LINE : LINE + 8])
    moves = [
        pltpu.make_async_copy(source, target, sems.at[n])
        for n, (source, target) in enumerate(zip(sources, targets))
    ]
    for move in moves:
        move.start()
    pack[MASK : MASK + 8] = jnp.full((8, LANES), order[0, 0], jnp.int32).astype(jnp.float32)
    for move in moves:
        move.wait()
    electrons, holes, first, second, twiddle, decay = copies
    values = density_spectra(electrons, holes, first, twiddle, second)
    found = moments(values, decay[0])
    for c in range(2):
        pack[c * ROWS : (c + 1) * ROWS] = values[:, c * LANES : (c + 1) * LANES]
        for way in range(2):
            row = SUMS + (way * 2 + c) * HALF
            pack[row : row + HALF] = found[way][c]


def hold_kernel(source, target):
    target[...] = source[...]


def straight_of(pack, rows):
    return jnp.broadcast_to(pack[MASK : MASK + 1], (rows, LANES)) < 0.5


def far_kernel(pack, electrons, holes, first, twiddle, second, decay, spectra, out):
    values = density_spectra(electrons, holes, first, twiddle, second)
    spectra[...] = values
    found = moments(values, decay[0])
    straight = straight_of(pack, HALF)
    for way in range(2):
        for c in range(2):
            row = SUMS + (way * 2 + c) * HALF
            near, far = pack[row : row + HALF], found[way][c]
            pair = (jnp.where(straight, near, far), jnp.where(straight, far, near))
            for p in range(2):
                for kl in range(2):
                    row = way * 8 + p * 4 + c * 2 + kl
                    out[pl.ds(row, PARTS, stride=16), :] = pair[p][kl * PARTS : (kl + 1) * PARTS]


def total(values):
    return jnp.sum(values, axis=0, keepdims=True)


def local_terms(pack, far, green, decay, local):
    straight = straight_of(pack, HALF)
    weight = [green[...]] + [green[...] * decay[n] for n in range(3)]
    own_values = jnp.concatenate([pack[0:ROWS], pack[ROWS : 2 * ROWS]], axis=1)
    far_values = far[...]
    density, field = {}, {}
    for c in range(2):
        near, distant = planes_of(own_values, c), planes_of(far_values, c)
        for x in range(PLANES):
            density[0, c, x] = jnp.where(straight, near[x], distant[x])
            density[1, c, x] = jnp.where(straight, distant[x], near[x])
    for p in range(2):
        for c in range(2):
            for x in range(PLANES):
                value = weight[0] * density[p, c, x]
                for other in range(PLANES):
                    if other != x:
                        value += weight[abs(x - other)] * density[p, c, other]
                field[p, c, x] = value
                local[p, x * HALF : (x + 1) * HALF, c * LANES : (c + 1) * LANES] = value
    zero = jnp.zeros((HALF, LANES), jnp.float32)
    terms = [zero, zero, zero, zero]
    for x in range(PLANES):
        for c in range(2):
            terms[0] += field[0, c, x] * density[0, c, x]
            terms[1] += field[1, c, x] * density[1, c, x]
            terms[2] += field[0, c, x] * density[1, c, x]
        terms[3] += field[0, 1, x] * density[1, 0, x] - field[0, 0, x] * density[1, 1, x]
    lane = lax.broadcasted_iota(jnp.int32, (1, LANES), 1)
    rows = []
    for x in range(PLANES):
        row = jnp.zeros((1, LANES), jnp.float32)
        for p in range(2):
            for c in range(2):
                value = jnp.broadcast_to(density[p, c, x][0:1, 0:1], (1, LANES))
                row = jnp.where(lane // 16 == p * 2 + c, value, row)
        rows.append(row)
    return jnp.concatenate(rows, axis=0), [total(t) for t in terms]


def screen_kernel(block, pack, far, green, decay, out, local):
    ends, inner = local_terms(pack, far, green, decay, local)
    step, close, near = (pack[PART + 8 * n : PART + 8 * n + 8] for n in range(3))
    right = [block[s, 0:8] for s in range(PARTS)]
    left = [block[s, 8:16] for s in range(PARTS)]
    from_right, from_left = right[0], left[PARTS - 1]
    for n in range(1, PARTS):
        from_right = from_right * step + right[n]
        from_left = from_left * step + left[PARTS - 1 - n]
    from_right, from_left = from_right * close, from_left * close
    effect = {}
    for n in range(PARTS):
        effect[0, n] = near * from_right
        effect[1, PARTS - 1 - n] = near * from_left
        from_right = from_right * step + right[n]
        from_left = from_left * step + left[PARTS - 1 - n]
    zero = jnp.zeros((8, LANES), jnp.float32)
    same, cross, swapped = zero, zero, zero
    for s in range(PARTS):
        for way, moment in ((0, left[s]), (1, right[s])):
            value = effect[way, s]
            out[s * STRIDE + way * 8 : s * STRIDE + way * 8 + 8] = value
            turned = jnp.concatenate([moment[4:8], moment[0:4]], axis=0)
            same += value * moment
            cross += value * turned
            swapped += value * jnp.concatenate([moment[6:8], moment[4:6], moment[0:4]], axis=0)
    terms = [
        total(same[0:4]),
        total(same[4:8]),
        total(cross[0:4]),
        total(swapped[2:4]) - total(swapped[0:2]),
    ]
    terms = jnp.concatenate([a + b for a, b in zip(inner, terms)], axis=0)
    terms += pltpu.roll(terms, LANES // 2, 1)
    lane = lax.broadcasted_iota(jnp.int32, (PLANES, LANES), 1)
    ends = jnp.where(lane < LANES // 2, ends, terms)
    for s in range(PARTS):
        out[s * STRIDE + 16 : s * STRIDE + 20] = ends


def field_kernel(block, local, decay, twiddle, third, fourth, uniform, pack, potential, coulomb):
    weight = [None, decay[0], decay[1], decay[2]]

    def effect(way, p, c):
        rows = [block[pl.ds(way * 8 + p * 4 + c * 2 + kl, PARTS, stride=STRIDE), :] for kl in range(2)]
        return jnp.concatenate(rows, axis=0)

    pairs = []
    for p in range(2):
        parts = []
        for c in range(2):
            right, left = effect(0, p, c), effect(1, p, c)
            planes = []
            for x in range(PLANES):
                value = local[p, x * HALF : (x + 1) * HALF, c * LANES : (c + 1) * LANES]
                value += right if x == 0 else right * weight[x]
                value += left if x == PLANES - 1 else left * weight[PLANES - 1 - x]
                planes.append(value)
            parts.append(jnp.concatenate(planes, axis=0))
        pairs.append(jnp.concatenate(parts, axis=1))
    mixed = dot_halves(halves(jnp.concatenate(pairs, axis=0)), (third[0], third[1]))
    columns = []
    for p in range(2):
        u_re, u_im = mixed[p * ROWS : (p + 1) * ROWS, :LANES], mixed[p * ROWS : (p + 1) * ROWS, LANES:]
        t_re = u_re * twiddle[0] - u_im * twiddle[1]
        t_im = u_im * twiddle[0] + u_re * twiddle[1]
        columns.append(jnp.concatenate([t_re, t_im], axis=0))
    ends = jnp.concatenate([block[STRIDE * s + 16 : STRIDE * s + 20] for s in range(PARTS)], axis=0)
    lane = lax.broadcasted_iota(jnp.int32, (NX, LANES), 1)
    plane = jnp.where(lane < LANES // 2, ends, 0.0)
    plane = plane - total(plane) * (1.0 / NX)
    own = dot(pack[LINE : LINE + 8, 0:NX], plane)
    lane = lax.broadcasted_iota(jnp.int32, (8, LANES), 1)
    shift = [
        jnp.where(
            lane < NZ,
            jnp.broadcast_to(own[:, 32 * p : 32 * p + 1], (8, LANES)),
            jnp.broadcast_to(own[:, 32 * p + 16 : 32 * p + 17], (8, LANES)),
        )
        for p in range(2)
    ]
    lane = lax.broadcasted_iota(jnp.int32, (HALF, LANES), 1)
    values = dot_halves((fourth[0], fourth[1]), halves(jnp.concatenate(columns, axis=1)))
    for p in range(2):
        for x in range(PLANES):
            re = values[x * HALF : (x + 1) * HALF, p * LANES : (p + 1) * LANES]
            im = values[ROWS + x * HALF : ROWS + (x + 1) * HALF, p * LANES : (p + 1) * LANES]
            even = jnp.where(lane < NZ, re, pltpu.roll(im, NZ, 1))
            odd = jnp.where(lane < NZ, pltpu.roll(re, NZ, 1), im)
            potential[p, x, pl.ds(0, HALF, stride=2), :] = even + shift[p][x : x + 1]
            potential[p, x, pl.ds(1, HALF, stride=2), :] = odd + shift[p][x : x + 1]
    line_all = jnp.concatenate([uniform[s, 0:PLANES, 0:NX] for s in range(PARTS)], axis=0)
    level = dot(line_all, plane)
    lane = lax.broadcasted_iota(jnp.int32, (1, LANES), 1)
    same = total(level * plane) * (1.0 / 16)
    cross = total(level * pltpu.roll(plane, 96, 1)) * (1.0 / 16)
    swapped = total(jnp.where(lane < 16, -level * pltpu.roll(plane, 80, 1), level * pltpu.roll(plane, 112, 1))) * (1.0 / 16)
    ahead = lane < 32
    extra = [jnp.where(ahead, same, 0.0), jnp.where(ahead, 0.0, same), jnp.where(ahead, cross, 0.0), jnp.where(ahead, swapped, 0.0)]
    sums = ends[0:PLANES]
    for s in range(1, PARTS):
        sums += ends[s * PLANES : (s + 1) * PLANES]
    sums = jnp.where(lane < LANES // 2, 0.0, sums) + jnp.concatenate(extra, axis=0)
    sums = jnp.sum(sums, axis=1, keepdims=True) * (1.0 / CELLS)
    c00, c11, re, im = (sums[k : k + 1] for k in range(4))
    row = lax.broadcasted_iota(jnp.int32, (2, 2), 0)
    col = lax.broadcasted_iota(jnp.int32, (2, 2), 1)
    coulomb[0] = jnp.where(row == col, jnp.where(row == 0, c00, c11), re)
    coulomb[1] = jnp.where(row == col, 0.0, jnp.where(row == 0, im, -im))


def full(memory_space=pltpu.VMEM):
    return pl.BlockSpec(memory_space=memory_space)


def call(kernel, name, out_shape, *operands, scalars=0, space=pltpu.VMEM, scratch=(), limit=32):
    specs = [full(pltpu.SMEM)] * scalars + [full(space)] * (len(operands) - scalars)
    several = isinstance(out_shape, (list, tuple))
    return pl.pallas_call(
        kernel,
        out_shape=out_shape,
        in_specs=specs,
        out_specs=[full()] * len(out_shape) if several else full(),
        scratch_shapes=scratch,
        compiler_params=pltpu.CompilerParams(vmem_limit_bytes=limit * 1024 * 1024),
        name=name,
    )(*operands)


def shape(*dims, dtype=jnp.float32):
    return jax.ShapeDtypeStruct(dims, dtype)


def tiled_states(states):
    bands = states.shape[1]
    parts = states.reshape(bands, 2, PLANES, HALF, LANES)
    return parts.transpose(0, 1, 3, 2, 4).reshape(bands, 2, ROWS, LANES)


def split_table(values):
    top = values.astype(ml_dtypes.bfloat16)
    rest = (values - top.astype(np.float32)).astype(ml_dtypes.bfloat16)
    return jnp.asarray(np.stack([top, rest]))


def shards(electrons, holes, pair_order):
    found = tables()
    t = {name: jnp.asarray(value) for name, value in found.items()}
    for name in ("first", "second", "third", "fourth"):
        t[name] = split_table(found[name])
    groups = lax.axis_size("blk")
    rank = lax.axis_index("space").astype(jnp.int32).reshape(1)
    previous = lax.ppermute(holes, "blk", [((i - 1) % groups, i) for i in range(groups)])
    e = tiled_states(electrons)
    spectra = shape(ROWS, 2 * LANES)
    h = tiled_states(holes)
    brought = (e, h, t["first"], t["second"], t["twiddle"], t["decay"])
    pack = call(
        own_kernel, "own_pair", shape(PACKED, LANES), rank, pair_order, *brought, t["parts"], t["uniform"],
        scalars=2, space=pltpu.HBM, limit=60,
        scratch=[pltpu.VMEM(x.shape, x.dtype) for x in brought] + [pltpu.SemaphoreType.DMA((8,))],
    )
    pack = call(hold_kernel, "hold", shape(PACKED, LANES), pack)
    far, sent = call(
        far_kernel, "far_pair", [spectra, shape(PARTS * 16, LANES)],
        pack, e, tiled_states(previous), t["first"], t["twiddle"], t["second"], t["decay"],
    )
    blocks = lax.all_to_all(sent.reshape(PARTS, 16, LANES), "space", split_axis=0, concat_axis=0, tiled=True)
    effects, local = call(
        screen_kernel, "screen", [shape(PARTS * STRIDE, LANES), shape(2, ROWS, 2 * LANES)],
        blocks, pack, far, t["green"], t["decay"],
    )
    effects = effects.reshape(PARTS, STRIDE // 4, 4, LANES)
    effects = lax.all_to_all(effects, "space", split_axis=0, concat_axis=0, tiled=True)
    potential, coulomb = call(
        field_kernel, "field", [shape(2, PLANES, NY, LANES), shape(2, 2, 2)],
        effects.reshape(PARTS * STRIDE, LANES), local, t["decay"], t["twiddle"], t["third"], t["fourth"], t["uniform"], pack,
    )
    return (potential[None], coulomb[None])


def solution(mesh):
    in_specs = (
        P("blk", None, None, "space", None),
        P("blk", None, None, "space", None),
        P("blk", None),
    )
    out_specs = (P("blk", None, "space", None, None), P("blk", None, None, None))
    return jax.shard_map(shards, mesh=mesh, in_specs=in_specs, out_specs=out_specs, check_vma=False)
```

```python
import math

import jax
import jax.numpy as jnp
import ml_dtypes
import numpy as np
from jax import lax
from jax.experimental import pallas as pl
from jax.experimental.pallas import tpu as pltpu
from jax.sharding import PartitionSpec as P

NX = 64
NY = 64
NZ = 64
CELLS = NX * NY * NZ
SCREENING = 0.01
PARTS = 16
PLANES = NX // PARTS
HALF = NY // 2
ROWS = HALF * PLANES
LANES = 128
SUMS, PART, LINE, MASK, LOCAL, TERM, PACKED = 256, 384, 408, 416, 424, 680, 688
STRIDE = 20


def turn(angles, sign):
    cosines, sines = np.cos(angles), sign * np.sin(angles)
    return np.array([[cosines, -sines], [sines, cosines]])


def tables():
    half, full = np.arange(HALF), np.arange(NY)
    two = np.arange(2)
    eye_x = np.eye(PLANES)
    order = np.array([2 * d + kl for kl in range(2) for d in range(PARTS)])
    rows = turn(2 * math.pi * (np.outer(order, half) % HALF) / HALF, -1)
    first = np.einsum("dckn,yx->dykcnx", rows, eye_x).reshape(2 * ROWS, 2 * ROWS)
    angles = 2 * math.pi / NY * order[None, :, None, None] * two[None, None, :, None]
    angles = np.broadcast_to(angles, (PLANES, HALF, 2, NZ)).reshape(ROWS, LANES)
    twiddle = np.stack([np.cos(angles), np.sin(angles)])
    depth = turn(2 * math.pi * (np.outer(full, full) % NZ) / NZ, -1)
    signs = np.array([[1.0, 1.0], [1.0, -1.0]])
    second = np.einsum("dckz,hb->cbzdhk", depth, signs).reshape(2 * LANES, 2 * LANES)
    term = 2.0 - 2.0 * np.cos(2 * math.pi * full / 64)
    excess = term[:, None] + term[None, :] + SCREENING
    kappa = 2.0 * np.arcsinh(0.5 * np.sqrt(excess))
    kappa = kappa.reshape(2, HALF, NZ).transpose(1, 0, 2).reshape(HALF, LANES)
    green = 1.0 / (2.0 * np.sinh(kappa)) / (NY * NZ)
    green[0, 0] = 0.0
    decay = np.stack([np.exp(-kappa * n)[order] for n in (1, 2, 3)])
    step = np.exp(-PLANES * kappa)
    close = 1.0 / (1.0 - np.exp(-NX * kappa))
    near = green * np.exp(-kappa)
    parts = np.stack([step, close, near]).reshape(3, PARTS, 1, 2, LANES)
    parts = np.broadcast_to(parts, (3, PARTS, 4, 2, LANES)).transpose(1, 0, 2, 3, 4).reshape(PARTS, 24, LANES)
    line = np.array([0.0] + [1.0 / (t + SCREENING) for t in term[1:]])
    along = np.cos(2 * math.pi * (np.outer(full, full) % NX) / NX) @ line / NX / (NY * NZ)
    lag = along[(full[:, None] - full[None, :]) % NX]
    uniform = np.zeros((PARTS, 8, LANES))
    uniform[:, :PLANES, :NX] = lag.reshape(PARTS, PLANES, NX)
    back = turn(2 * math.pi * (np.outer(full, full) % NZ) / NZ, 1)
    third = np.einsum("dczk,hb->chkdbz", back, signs).reshape(2 * LANES, 2 * LANES)
    columns = turn(2 * math.pi * (np.outer(half, order) % HALF) / HALF, 1)
    fourth = np.einsum("dcnk,yx->dyncxk", columns, eye_x).reshape(2 * ROWS, 2 * ROWS)
    names = ("first", "twiddle", "second", "green", "decay", "parts", "uniform", "third", "fourth")
    values = (first, twiddle, second, green[order], decay, parts, uniform, third, fourth)
    return {n: np.ascontiguousarray(v, dtype=np.float32) for n, v in zip(names, values)}


def dot(a, b):
    return jnp.dot(a, b, precision=lax.Precision.HIGHEST, preferred_element_type=jnp.float32)


def halves(values):
    top = values.astype(jnp.bfloat16)
    return top, (values - top.astype(jnp.float32)).astype(jnp.bfloat16)


def dot_halves(a, b):
    def product(x, y):
        return jnp.dot(x, y, preferred_element_type=jnp.float32)

    return product(a[0], b[0]) + (product(a[0], b[1]) + product(a[1], b[0]))


def left_halves(table, values):
    parts = halves(values)
    width = values.shape[1]
    both = jnp.dot(table[0], jnp.concatenate(parts, axis=1), preferred_element_type=jnp.float32)
    rest = jnp.dot(table[1], parts[0], preferred_element_type=jnp.float32)
    return both[:, :width] + (both[:, width:] + rest)


def right_halves(values, table):
    parts = halves(values)
    height = values.shape[0]
    both = jnp.dot(jnp.concatenate(parts, axis=0), table[0], preferred_element_type=jnp.float32)
    rest = jnp.dot(parts[0], table[1], preferred_element_type=jnp.float32)
    return both[:height] + (both[height:] + rest)


def with_first_row(values, rows):
    first = lax.broadcasted_iota(jnp.int32, (8, values.shape[1]), 0) == 0
    pieces = []
    for x in range(PLANES):
        own = values[x * HALF : (x + 1) * HALF]
        pieces += [jnp.where(first, rows[x : x + 1], own[:8]), own[8:]]
    return jnp.concatenate(pieces, axis=0)


def density_spectra(electrons, holes, first, twiddle, second):
    real = jnp.zeros((ROWS, LANES), jnp.float32)
    imag = jnp.zeros((ROWS, LANES), jnp.float32)
    for band in range(electrons.shape[0]):
        e_re = electrons[band, 0].astype(jnp.float32)
        e_im = electrons[band, 1].astype(jnp.float32)
        h_re = holes[band, 0].astype(jnp.float32)
        h_im = holes[band, 1].astype(jnp.float32)
        real += e_re * h_re + e_im * h_im
        imag += e_re * h_im - e_im * h_re
    around, column, level = [], [], []
    for part in (real, imag):
        rows = part[0:8]
        for k in range(1, ROWS // 8):
            rows = rows + part[k * 8 : k * 8 + 8]
        mean = (rows[0:4] + rows[4:8]) * (1.0 / HALF)
        grand = jnp.sum(mean, axis=1, keepdims=True) * (1.0 / LANES)
        around.append(part - jnp.concatenate([mean] * HALF, axis=0))
        column.append((mean - grand) * HALF)
        level.append(grand * (NY * NZ))
    mixed = left_halves(first, jnp.concatenate(around, axis=0))
    u_re, u_im = mixed[:ROWS], mixed[ROWS:]
    t_re = with_first_row(u_re * twiddle[0] + u_im * twiddle[1], column[0])
    t_im = with_first_row(u_im * twiddle[0] - u_re * twiddle[1], column[1])
    values = right_halves(jnp.concatenate([t_re, t_im], axis=1), second)
    lane = lax.broadcasted_iota(jnp.int32, (PLANES, LANES), 1)
    parts = []
    for c in range(2):
        part = values[:, c * LANES : (c + 1) * LANES]
        rows = jnp.concatenate([part[x * HALF : x * HALF + 1] for x in range(PLANES)], axis=0)
        parts.append(with_first_row(part, rows + jnp.where(lane == 0, level[c], 0.0)))
    return jnp.concatenate(parts, axis=1)


def planes_of(spectra, c):
    return [spectra[x * HALF : (x + 1) * HALF, c * LANES : (c + 1) * LANES] for x in range(PLANES)]


def moments(spectra, decay):
    found = [[None, None], [None, None]]
    for c in range(2):
        planes = planes_of(spectra, c)
        for way, run in enumerate((planes, planes[::-1])):
            total = run[0]
            for plane in run[1:]:
                total = total * decay + plane
            found[way][c] = total
    return found


def total(values):
    return jnp.sum(values, axis=0, keepdims=True)


def local_fields(values, green, decay):
    weight = [green[...]] + [green[...] * decay[n] for n in range(3)]
    density, field = {}, {}
    for c in range(2):
        planes = planes_of(values, c)
        for x in range(PLANES):
            value = weight[0] * planes[x]
            for other in range(PLANES):
                if other != x:
                    value += weight[abs(x - other)] * planes[other]
            density[c, x], field[c, x] = planes[x], value
    return density, field


def same_term(density, field):
    return total(sum(field[key] * density[key] for key in field))


def own_kernel(rank, order, *refs):
    sources, pack, copies, sems = refs[:9], refs[9], refs[10:17], refs[17]
    me = rank[0]
    sources = sources[:7] + (sources[7].at[me], sources[8].at[me])
    targets = copies + (pack.at[PART : PART + 24], pack.at[LINE : LINE + 8])
    moves = [
        pltpu.make_async_copy(source, target, sems.at[n])
        for n, (source, target) in enumerate(zip(sources, targets))
    ]
    for move in moves:
        move.start()
    pack[MASK : MASK + 8] = jnp.full((8, LANES), order[0, 0], jnp.int32).astype(jnp.float32)
    for move in moves:
        move.wait()
    electrons, holes, first, second, twiddle, decay, green = copies
    values = density_spectra(electrons, holes, first, twiddle, second)
    found = moments(values, decay[0])
    for c in range(2):
        pack[c * ROWS : (c + 1) * ROWS] = values[:, c * LANES : (c + 1) * LANES]
        for way in range(2):
            row = SUMS + (way * 2 + c) * HALF
            pack[row : row + HALF] = found[way][c]
    density, field = local_fields(values, green, decay)
    for c in range(2):
        for x in range(PLANES):
            row = LOCAL + c * ROWS + x * HALF
            pack[row : row + HALF] = field[c, x]
    pack[TERM : TERM + 8] = jnp.broadcast_to(same_term(density, field), (8, LANES))


def hold_kernel(source, target):
    target[...] = source[...]


def far_kernel(pack, electrons, holes, first, twiddle, second, decay, spectra, out):
    values = density_spectra(electrons, holes, first, twiddle, second)
    spectra[...] = values
    found = moments(values, decay[0])
    for way in range(2):
        for c in range(2):
            row = SUMS + (way * 2 + c) * HALF
            pair = (pack[row : row + HALF], found[way][c])
            for p in range(2):
                for kl in range(2):
                    row = way * 8 + p * 4 + c * 2 + kl
                    out[pl.ds(row, PARTS, stride=16), :] = pair[p][kl * PARTS : (kl + 1) * PARTS]


def local_terms(pack, far, green, decay, local):
    far_density, far_field = local_fields(far[...], green, decay)
    density, field = {}, {}
    for c in range(2):
        for x in range(PLANES):
            row = c * ROWS + x * HALF
            density[0, c, x], field[0, c, x] = pack[row : row + HALF], pack[LOCAL + row : LOCAL + row + HALF]
            density[1, c, x] = far_density[c, x]
            local[x * HALF : (x + 1) * HALF, c * LANES : (c + 1) * LANES] = far_field[c, x]
    cross = jnp.zeros((HALF, LANES), jnp.float32)
    swapped = jnp.zeros((HALF, LANES), jnp.float32)
    for x in range(PLANES):
        for c in range(2):
            cross += field[0, c, x] * density[1, c, x]
        swapped += field[0, 1, x] * density[1, 0, x] - field[0, 0, x] * density[1, 1, x]
    terms = [pack[TERM : TERM + 1], same_term(far_density, far_field), total(cross), total(swapped)]
    lane = lax.broadcasted_iota(jnp.int32, (1, LANES), 1)
    rows = []
    for x in range(PLANES):
        row = jnp.zeros((1, LANES), jnp.float32)
        for p in range(2):
            for c in range(2):
                value = jnp.broadcast_to(density[p, c, x][0:1, 0:1], (1, LANES))
                row = jnp.where(lane // 16 == p * 2 + c, value, row)
        rows.append(row)
    return jnp.concatenate(rows, axis=0), terms


def screen_kernel(block, pack, far, green, decay, out, local):
    ends, inner = local_terms(pack, far, green, decay, local)
    step, close, near = (pack[PART + 8 * n : PART + 8 * n + 8] for n in range(3))
    right = [block[s, 0:8] for s in range(PARTS)]
    left = [block[s, 8:16] for s in range(PARTS)]
    from_right, from_left = right[0], left[PARTS - 1]
    for n in range(1, PARTS):
        from_right = from_right * step + right[n]
        from_left = from_left * step + left[PARTS - 1 - n]
    from_right, from_left = from_right * close, from_left * close
    effect = {}
    for n in range(PARTS):
        effect[0, n] = near * from_right
        effect[1, PARTS - 1 - n] = near * from_left
        from_right = from_right * step + right[n]
        from_left = from_left * step + left[PARTS - 1 - n]
    zero = jnp.zeros((8, LANES), jnp.float32)
    same, cross, swapped = zero, zero, zero
    for s in range(PARTS):
        for way, moment in ((0, left[s]), (1, right[s])):
            value = effect[way, s]
            out[s * STRIDE + way * 8 : s * STRIDE + way * 8 + 8] = value
            turned = jnp.concatenate([moment[4:8], moment[0:4]], axis=0)
            same += value * moment
            cross += value * turned
            swapped += value * jnp.concatenate([moment[6:8], moment[4:6], moment[0:4]], axis=0)
    terms = [
        total(same[0:4]),
        total(same[4:8]),
        total(cross[0:4]),
        total(swapped[2:4]) - total(swapped[0:2]),
    ]
    terms = jnp.concatenate([a + b for a, b in zip(inner, terms)], axis=0)
    terms += pltpu.roll(terms, LANES // 2, 1)
    lane = lax.broadcasted_iota(jnp.int32, (PLANES, LANES), 1)
    ends = jnp.where(lane < LANES // 2, ends, terms)
    for s in range(PARTS):
        out[s * STRIDE + 16 : s * STRIDE + 20] = ends


def field_kernel(block, local, decay, twiddle, third, fourth, uniform, pack, potential, coulomb):
    weight = [None, decay[0], decay[1], decay[2]]
    first = jnp.clip(jnp.max(pack[MASK : MASK + 1, 0:1]).astype(jnp.int32), 0, 1)

    def effect(way, p, c):
        rows = [block[pl.ds(way * 8 + p * 4 + c * 2 + kl, PARTS, stride=STRIDE), :] for kl in range(2)]
        return jnp.concatenate(rows, axis=0)

    pairs = []
    for p in range(2):
        parts = []
        for c in range(2):
            right, left = effect(0, p, c), effect(1, p, c)
            planes = []
            for x in range(PLANES):
                if p == 0:
                    row = LOCAL + c * ROWS + x * HALF
                    value = pack[row : row + HALF]
                else:
                    value = local[x * HALF : (x + 1) * HALF, c * LANES : (c + 1) * LANES]
                value += right if x == 0 else right * weight[x]
                value += left if x == PLANES - 1 else left * weight[PLANES - 1 - x]
                planes.append(value)
            parts.append(jnp.concatenate(planes, axis=0))
        pairs.append(jnp.concatenate(parts, axis=1))
    mixed = dot_halves(halves(jnp.concatenate(pairs, axis=0)), (third[0], third[1]))
    columns = []
    for p in range(2):
        u_re, u_im = mixed[p * ROWS : (p + 1) * ROWS, :LANES], mixed[p * ROWS : (p + 1) * ROWS, LANES:]
        t_re = u_re * twiddle[0] - u_im * twiddle[1]
        t_im = u_im * twiddle[0] + u_re * twiddle[1]
        columns.append(jnp.concatenate([t_re, t_im], axis=0))
    ends = jnp.concatenate([block[STRIDE * s + 16 : STRIDE * s + 20] for s in range(PARTS)], axis=0)
    lane = lax.broadcasted_iota(jnp.int32, (NX, LANES), 1)
    plane = jnp.where(lane < LANES // 2, ends, 0.0)
    plane = plane - total(plane) * (1.0 / NX)
    own = dot(pack[LINE : LINE + 8, 0:NX], plane)
    lane = lax.broadcasted_iota(jnp.int32, (8, LANES), 1)
    shift = [
        jnp.where(
            lane < NZ,
            jnp.broadcast_to(own[:, 32 * p : 32 * p + 1], (8, LANES)),
            jnp.broadcast_to(own[:, 32 * p + 16 : 32 * p + 17], (8, LANES)),
        )
        for p in range(2)
    ]
    lane = lax.broadcasted_iota(jnp.int32, (HALF, LANES), 1)
    values = dot_halves((fourth[0], fourth[1]), halves(jnp.concatenate(columns, axis=1)))
    for p in range(2):
        place = first if p == 0 else 1 - first
        for x in range(PLANES):
            re = values[x * HALF : (x + 1) * HALF, p * LANES : (p + 1) * LANES]
            im = values[ROWS + x * HALF : ROWS + (x + 1) * HALF, p * LANES : (p + 1) * LANES]
            even = jnp.where(lane < NZ, re, pltpu.roll(im, NZ, 1))
            odd = jnp.where(lane < NZ, pltpu.roll(re, NZ, 1), im)
            potential[place, x, pl.ds(0, HALF, stride=2), :] = even + shift[p][x : x + 1]
            potential[place, x, pl.ds(1, HALF, stride=2), :] = odd + shift[p][x : x + 1]
    line_all = jnp.concatenate([uniform[s, 0:PLANES, 0:NX] for s in range(PARTS)], axis=0)
    level = dot(line_all, plane)
    lane = lax.broadcasted_iota(jnp.int32, (1, LANES), 1)
    same = total(level * plane) * (1.0 / 16)
    cross = total(level * pltpu.roll(plane, 96, 1)) * (1.0 / 16)
    swapped = total(jnp.where(lane < 16, -level * pltpu.roll(plane, 80, 1), level * pltpu.roll(plane, 112, 1))) * (1.0 / 16)
    ahead = lane < 32
    extra = [jnp.where(ahead, same, 0.0), jnp.where(ahead, 0.0, same), jnp.where(ahead, cross, 0.0), jnp.where(ahead, swapped, 0.0)]
    sums = ends[0:PLANES]
    for s in range(1, PARTS):
        sums += ends[s * PLANES : (s + 1) * PLANES]
    sums = jnp.where(lane < LANES // 2, 0.0, sums) + jnp.concatenate(extra, axis=0)
    sums = jnp.sum(sums, axis=1, keepdims=True) * (1.0 / CELLS)
    own, far, re, im = (sums[k : k + 1] for k in range(4))
    straight = pack[MASK : MASK + 1, 0:1] < 0.5
    c00, c11, im = jnp.where(straight, own, far), jnp.where(straight, far, own), jnp.where(straight, im, -im)
    row = lax.broadcasted_iota(jnp.int32, (2, 2), 0)
    col = lax.broadcasted_iota(jnp.int32, (2, 2), 1)
    coulomb[0] = jnp.where(row == col, jnp.where(row == 0, c00, c11), re)
    coulomb[1] = jnp.where(row == col, 0.0, jnp.where(row == 0, im, -im))


def full(memory_space=pltpu.VMEM):
    return pl.BlockSpec(memory_space=memory_space)


def call(kernel, name, out_shape, *operands, scalars=0, space=pltpu.VMEM, scratch=(), limit=32):
    specs = [full(pltpu.SMEM)] * scalars + [full(space)] * (len(operands) - scalars)
    several = isinstance(out_shape, (list, tuple))
    return pl.pallas_call(
        kernel,
        out_shape=out_shape,
        in_specs=specs,
        out_specs=[full()] * len(out_shape) if several else full(),
        scratch_shapes=scratch,
        compiler_params=pltpu.CompilerParams(vmem_limit_bytes=limit * 1024 * 1024),
        name=name,
    )(*operands)


def shape(*dims, dtype=jnp.float32):
    return jax.ShapeDtypeStruct(dims, dtype)


def tiled_states(states):
    bands = states.shape[1]
    parts = states.reshape(bands, 2, PLANES, HALF, LANES)
    return parts.transpose(0, 1, 3, 2, 4).reshape(bands, 2, ROWS, LANES)


def split_table(values):
    top = values.astype(ml_dtypes.bfloat16)
    rest = (values - top.astype(np.float32)).astype(ml_dtypes.bfloat16)
    return jnp.asarray(np.stack([top, rest]))


def shards(electrons, holes, pair_order):
    found = tables()
    t = {name: jnp.asarray(value) for name, value in found.items()}
    for name in ("first", "second", "third", "fourth"):
        t[name] = split_table(found[name])
    groups = lax.axis_size("blk")
    rank = lax.axis_index("space").astype(jnp.int32).reshape(1)
    previous = lax.ppermute(holes, "blk", [((i - 1) % groups, i) for i in range(groups)])
    e = tiled_states(electrons)
    spectra = shape(ROWS, 2 * LANES)
    h = tiled_states(holes)
    brought = (e, h, t["first"], t["second"], t["twiddle"], t["decay"], t["green"])
    pack = call(
        own_kernel, "own_pair", shape(PACKED, LANES), rank, pair_order, *brought, t["parts"], t["uniform"],
        scalars=2, space=pltpu.HBM, limit=60,
        scratch=[pltpu.VMEM(x.shape, x.dtype) for x in brought] + [pltpu.SemaphoreType.DMA((9,))],
    )
    pack = call(hold_kernel, "hold", shape(PACKED, LANES), pack)
    far, sent = call(
        far_kernel, "far_pair", [spectra, shape(PARTS * 16, LANES)],
        pack, e, tiled_states(previous), t["first"], t["twiddle"], t["second"], t["decay"],
    )
    blocks = lax.all_to_all(sent.reshape(PARTS, 16, LANES), "space", split_axis=0, concat_axis=0, tiled=True)
    effects, local = call(
        screen_kernel, "screen", [shape(PARTS * STRIDE, LANES), shape(ROWS, 2 * LANES)],
        blocks, pack, far, t["green"], t["decay"],
    )
    effects = effects.reshape(PARTS, STRIDE // 4, 4, LANES)
    effects = lax.all_to_all(effects, "space", split_axis=0, concat_axis=0, tiled=True)
    potential, coulomb = call(
        field_kernel, "field", [shape(2, PLANES, NY, LANES), shape(2, 2, 2)],
        effects.reshape(PARTS * STRIDE, LANES), local, t["decay"], t["twiddle"], t["third"], t["fourth"], t["uniform"], pack,
    )
    return (potential[None], coulomb[None])


def solution(mesh):
    in_specs = (
        P("blk", None, None, "space", None),
        P("blk", None, None, "space", None),
        P("blk", None),
    )
    out_specs = (P("blk", None, "space", None, None), P("blk", None, None, None))
    return jax.shard_map(shards, mesh=mesh, in_specs=in_specs, out_specs=out_specs, check_vma=False)
```

```python
import math

import jax
import jax.numpy as jnp
import ml_dtypes
import numpy as np
from jax import lax
from jax.experimental import pallas as pl
from jax.experimental.pallas import tpu as pltpu
from jax.sharding import PartitionSpec as P

NX = 64
NY = 64
NZ = 64
CELLS = NX * NY * NZ
SCREENING = 0.01
PARTS = 16
PLANES = NX // PARTS
HALF = NY // 2
ROWS = HALF * PLANES
LANES = 128
SUMS, PART, LINE, MASK, PACKED = 256, 384, 408, 416, 424
STRIDE = 20


def turn(angles, sign):
    cosines, sines = np.cos(angles), sign * np.sin(angles)
    return np.array([[cosines, -sines], [sines, cosines]])


def tables():
    half, full = np.arange(HALF), np.arange(NY)
    two = np.arange(2)
    eye_x = np.eye(PLANES)
    order = np.array([2 * d + kl for kl in range(2) for d in range(PARTS)])
    rows = turn(2 * math.pi * (np.outer(order, half) % HALF) / HALF, -1)
    first = np.einsum("dckn,yx->dykcnx", rows, eye_x).reshape(2 * ROWS, 2 * ROWS)
    angles = 2 * math.pi / NY * order[None, :, None, None] * two[None, None, :, None]
    angles = np.broadcast_to(angles, (PLANES, HALF, 2, NZ)).reshape(ROWS, LANES)
    twiddle = np.stack([np.cos(angles), np.sin(angles)])
    depth = turn(2 * math.pi * (np.outer(full, full) % NZ) / NZ, -1)
    signs = np.array([[1.0, 1.0], [1.0, -1.0]])
    second = np.einsum("dckz,hb->cbzdhk", depth, signs).reshape(2 * LANES, 2 * LANES)
    term = 2.0 - 2.0 * np.cos(2 * math.pi * full / 64)
    excess = term[:, None] + term[None, :] + SCREENING
    kappa = 2.0 * np.arcsinh(0.5 * np.sqrt(excess))
    kappa = kappa.reshape(2, HALF, NZ).transpose(1, 0, 2).reshape(HALF, LANES)
    green = 1.0 / (2.0 * np.sinh(kappa)) / (NY * NZ)
    green[0, 0] = 0.0
    decay = np.stack([np.exp(-kappa * n)[order] for n in (1, 2, 3)])
    step = np.exp(-PLANES * kappa)
    close = 1.0 / (1.0 - np.exp(-NX * kappa))
    near = green * np.exp(-kappa)
    parts = np.stack([step, close, near]).reshape(3, PARTS, 1, 2, LANES)
    parts = np.broadcast_to(parts, (3, PARTS, 4, 2, LANES)).transpose(1, 0, 2, 3, 4).reshape(PARTS, 24, LANES)
    line = np.array([0.0] + [1.0 / (t + SCREENING) for t in term[1:]])
    along = np.cos(2 * math.pi * (np.outer(full, full) % NX) / NX) @ line / NX / (NY * NZ)
    lag = along[(full[:, None] - full[None, :]) % NX]
    uniform = np.zeros((PARTS, 8, LANES))
    uniform[:, :PLANES, :NX] = lag.reshape(PARTS, PLANES, NX)
    back = turn(2 * math.pi * (np.outer(full, full) % NZ) / NZ, 1)
    third = np.einsum("dczk,hb->chkdbz", back, signs).reshape(2 * LANES, 2 * LANES)
    columns = turn(2 * math.pi * (np.outer(half, order) % HALF) / HALF, 1)
    fourth = np.einsum("dcnk,yx->dyncxk", columns, eye_x).reshape(2 * ROWS, 2 * ROWS)
    names = ("first", "twiddle", "second", "green", "decay", "parts", "uniform", "third", "fourth")
    values = (first, twiddle, second, green[order], decay, parts, uniform, third, fourth)
    return {n: np.ascontiguousarray(v, dtype=np.float32) for n, v in zip(names, values)}


def dot(a, b):
    return jnp.dot(a, b, precision=lax.Precision.HIGHEST, preferred_element_type=jnp.float32)


def halves(values):
    top = values.astype(jnp.bfloat16)
    return top, (values - top.astype(jnp.float32)).astype(jnp.bfloat16)


def dot_halves(a, b):
    def product(x, y):
        return jnp.dot(x, y, preferred_element_type=jnp.float32)

    return product(a[0], b[0]) + (product(a[0], b[1]) + product(a[1], b[0]))


def left_halves(table, values):
    parts = halves(values)
    width = values.shape[1]
    both = jnp.dot(table[0], jnp.concatenate(parts, axis=1), preferred_element_type=jnp.float32)
    rest = jnp.dot(table[1], parts[0], preferred_element_type=jnp.float32)
    return both[:, :width] + (both[:, width:] + rest)


def right_halves(values, table):
    parts = halves(values)
    height = values.shape[0]
    both = jnp.dot(jnp.concatenate(parts, axis=0), table[0], preferred_element_type=jnp.float32)
    rest = jnp.dot(parts[0], table[1], preferred_element_type=jnp.float32)
    return both[:height] + (both[height:] + rest)


def with_first_row(values, rows):
    first = lax.broadcasted_iota(jnp.int32, (8, values.shape[1]), 0) == 0
    pieces = []
    for x in range(PLANES):
        own = values[x * HALF : (x + 1) * HALF]
        pieces += [jnp.where(first, rows[x : x + 1], own[:8]), own[8:]]
    return jnp.concatenate(pieces, axis=0)


def density_spectra(electrons, holes, first, twiddle, second):
    real = jnp.zeros((ROWS, LANES), jnp.float32)
    imag = jnp.zeros((ROWS, LANES), jnp.float32)
    for band in range(electrons.shape[0]):
        e_re = electrons[band, 0].astype(jnp.float32)
        e_im = electrons[band, 1].astype(jnp.float32)
        h_re = holes[band, 0].astype(jnp.float32)
        h_im = holes[band, 1].astype(jnp.float32)
        real += e_re * h_re + e_im * h_im
        imag += e_re * h_im - e_im * h_re
    around, column, level = [], [], []
    for part in (real, imag):
        rows = part[0:8]
        for k in range(1, ROWS // 8):
            rows = rows + part[k * 8 : k * 8 + 8]
        mean = (rows[0:4] + rows[4:8]) * (1.0 / HALF)
        grand = jnp.sum(mean, axis=1, keepdims=True) * (1.0 / LANES)
        around.append(part - jnp.concatenate([mean] * HALF, axis=0))
        column.append((mean - grand) * HALF)
        level.append(grand * (NY * NZ))
    mixed = left_halves(first, jnp.concatenate(around, axis=0))
    u_re, u_im = mixed[:ROWS], mixed[ROWS:]
    t_re = with_first_row(u_re * twiddle[0] + u_im * twiddle[1], column[0])
    t_im = with_first_row(u_im * twiddle[0] - u_re * twiddle[1], column[1])
    values = right_halves(jnp.concatenate([t_re, t_im], axis=1), second)
    lane = lax.broadcasted_iota(jnp.int32, (PLANES, LANES), 1)
    parts = []
    for c in range(2):
        part = values[:, c * LANES : (c + 1) * LANES]
        rows = jnp.concatenate([part[x * HALF : x * HALF + 1] for x in range(PLANES)], axis=0)
        parts.append(with_first_row(part, rows + jnp.where(lane == 0, level[c], 0.0)))
    return jnp.concatenate(parts, axis=1)


def planes_of(spectra, c):
    return [spectra[x * HALF : (x + 1) * HALF, c * LANES : (c + 1) * LANES] for x in range(PLANES)]


def moments(spectra, decay):
    found = [[None, None], [None, None]]
    for c in range(2):
        planes = planes_of(spectra, c)
        for way, run in enumerate((planes, planes[::-1])):
            total = run[0]
            for plane in run[1:]:
                total = total * decay + plane
            found[way][c] = total
    return found


def own_kernel(rank, order, *refs):
    sources, pack, copies, sems = refs[:8], refs[8], refs[9:15], refs[15]
    me = rank[0]
    sources = sources[:6] + (sources[6].at[me], sources[7].at[me])
    targets = copies + (pack.at[PART : PART + 24], pack.at[LINE : LINE + 8])
    moves = [
        pltpu.make_async_copy(source, target, sems.at[n])
        for n, (source, target) in enumerate(zip(sources, targets))
    ]
    for move in moves:
        move.start()
    pack[MASK : MASK + 8] = jnp.full((8, LANES), order[0, 0], jnp.int32).astype(jnp.float32)
    for move in moves:
        move.wait()
    electrons, holes, first, second, twiddle, decay = copies
    values = density_spectra(electrons, holes, first, twiddle, second)
    found = moments(values, decay[0])
    for c in range(2):
        pack[c * ROWS : (c + 1) * ROWS] = values[:, c * LANES : (c + 1) * LANES]
        for way in range(2):
            row = SUMS + (way * 2 + c) * HALF
            pack[row : row + HALF] = found[way][c]


def hold_kernel(source, target):
    target[...] = source[...]


def straight_of(pack, rows):
    return jnp.broadcast_to(pack[MASK : MASK + 1], (rows, LANES)) < 0.5


def far_kernel(pack, electrons, holes, first, twiddle, second, decay, spectra, out):
    values = density_spectra(electrons, holes, first, twiddle, second)
    spectra[...] = values
    found = moments(values, decay[0])
    straight = straight_of(pack, HALF)
    for way in range(2):
        for c in range(2):
            row = SUMS + (way * 2 + c) * HALF
            near, far = pack[row : row + HALF], found[way][c]
            pair = (jnp.where(straight, near, far), jnp.where(straight, far, near))
            for p in range(2):
                for kl in range(2):
                    row = way * 8 + p * 4 + c * 2 + kl
                    out[pl.ds(row, PARTS, stride=16), :] = pair[p][kl * PARTS : (kl + 1) * PARTS]


def total(values):
    return jnp.sum(values, axis=0, keepdims=True)


def local_terms(pack, far, green, decay, local):
    straight = straight_of(pack, HALF)
    weight = [green[...]] + [green[...] * decay[n] for n in range(3)]
    own_values = jnp.concatenate([pack[0:ROWS], pack[ROWS : 2 * ROWS]], axis=1)
    far_values = far[...]
    density, field = {}, {}
    for c in range(2):
        near, distant = planes_of(own_values, c), planes_of(far_values, c)
        for x in range(PLANES):
            density[0, c, x] = jnp.where(straight, near[x], distant[x])
            density[1, c, x] = jnp.where(straight, distant[x], near[x])
    for p in range(2):
        for c in range(2):
            for x in range(PLANES):
                value = weight[0] * density[p, c, x]
                for other in range(PLANES):
                    if other != x:
                        value += weight[abs(x - other)] * density[p, c, other]
                field[p, c, x] = value
                local[p, x * HALF : (x + 1) * HALF, c * LANES : (c + 1) * LANES] = value
    zero = jnp.zeros((HALF, LANES), jnp.float32)
    terms = [zero, zero, zero, zero]
    for x in range(PLANES):
        for c in range(2):
            terms[0] += field[0, c, x] * density[0, c, x]
            terms[1] += field[1, c, x] * density[1, c, x]
            terms[2] += field[0, c, x] * density[1, c, x]
        terms[3] += field[0, 1, x] * density[1, 0, x] - field[0, 0, x] * density[1, 1, x]
    lane = lax.broadcasted_iota(jnp.int32, (1, LANES), 1)
    rows = []
    for x in range(PLANES):
        row = jnp.zeros((1, LANES), jnp.float32)
        for p in range(2):
            for c in range(2):
                value = jnp.broadcast_to(density[p, c, x][0:1, 0:1], (1, LANES))
                row = jnp.where(lane // 16 == p * 2 + c, value, row)
        rows.append(row)
    return jnp.concatenate(rows, axis=0), [total(t) for t in terms]


def screen_kernel(block, pack, far, green, decay, out, local):
    ends, inner = local_terms(pack, far, green, decay, local)
    step, close, near = (pack[PART + 8 * n : PART + 8 * n + 8] for n in range(3))
    right = [block[s, 0:8] for s in range(PARTS)]
    left = [block[s, 8:16] for s in range(PARTS)]
    from_right, from_left = right[0], left[PARTS - 1]
    for n in range(1, PARTS):
        from_right = from_right * step + right[n]
        from_left = from_left * step + left[PARTS - 1 - n]
    from_right, from_left = from_right * close, from_left * close
    effect = {}
    for n in range(PARTS):
        effect[0, n] = near * from_right
        effect[1, PARTS - 1 - n] = near * from_left
        from_right = from_right * step + right[n]
        from_left = from_left * step + left[PARTS - 1 - n]
    zero = jnp.zeros((8, LANES), jnp.float32)
    same, cross, swapped = zero, zero, zero
    for s in range(PARTS):
        for way, moment in ((0, left[s]), (1, right[s])):
            value = effect[way, s]
            out[s * STRIDE + way * 8 : s * STRIDE + way * 8 + 8] = value
            turned = jnp.concatenate([moment[4:8], moment[0:4]], axis=0)
            same += value * moment
            cross += value * turned
            swapped += value * jnp.concatenate([moment[6:8], moment[4:6], moment[0:4]], axis=0)
    terms = [
        total(same[0:4]),
        total(same[4:8]),
        total(cross[0:4]),
        total(swapped[2:4]) - total(swapped[0:2]),
    ]
    terms = jnp.concatenate([a + b for a, b in zip(inner, terms)], axis=0)
    terms += pltpu.roll(terms, LANES // 2, 1)
    lane = lax.broadcasted_iota(jnp.int32, (PLANES, LANES), 1)
    ends = jnp.where(lane < LANES // 2, ends, terms)
    for s in range(PARTS):
        out[s * STRIDE + 16 : s * STRIDE + 20] = ends


def field_kernel(block, local, decay, twiddle, third, fourth, uniform, pack, potential, coulomb):
    weight = [None, decay[0], decay[1], decay[2]]

    def effect(way, p, c):
        rows = [block[pl.ds(way * 8 + p * 4 + c * 2 + kl, PARTS, stride=STRIDE), :] for kl in range(2)]
        return jnp.concatenate(rows, axis=0)

    pairs = []
    for p in range(2):
        parts = []
        for c in range(2):
            right, left = effect(0, p, c), effect(1, p, c)
            planes = []
            for x in range(PLANES):
                value = local[p, x * HALF : (x + 1) * HALF, c * LANES : (c + 1) * LANES]
                value += right if x == 0 else right * weight[x]
                value += left if x == PLANES - 1 else left * weight[PLANES - 1 - x]
                planes.append(value)
            parts.append(jnp.concatenate(planes, axis=0))
        pairs.append(jnp.concatenate(parts, axis=1))
    mixed = dot_halves(halves(jnp.concatenate(pairs, axis=0)), (third[0], third[1]))
    columns = []
    for p in range(2):
        u_re, u_im = mixed[p * ROWS : (p + 1) * ROWS, :LANES], mixed[p * ROWS : (p + 1) * ROWS, LANES:]
        t_re = u_re * twiddle[0] - u_im * twiddle[1]
        t_im = u_im * twiddle[0] + u_re * twiddle[1]
        columns.append(jnp.concatenate([t_re, t_im], axis=0))
    ends = jnp.concatenate([block[STRIDE * s + 16 : STRIDE * s + 20] for s in range(PARTS)], axis=0)
    lane = lax.broadcasted_iota(jnp.int32, (NX, LANES), 1)
    plane = jnp.where(lane < LANES // 2, ends, 0.0)
    plane = plane - total(plane) * (1.0 / NX)
    lags = [uniform[s, 0:PLANES, 0:NX] for s in range(PARTS)] + [pack[LINE : LINE + 8, 0:NX]]
    level = dot(jnp.concatenate(lags, axis=0), plane)
    level, own = level[:NX], level[NX:]
    lane = lax.broadcasted_iota(jnp.int32, (8, LANES), 1)
    shift = [
        jnp.where(
            lane < NZ,
            jnp.broadcast_to(own[:, 32 * p : 32 * p + 1], (8, LANES)),
            jnp.broadcast_to(own[:, 32 * p + 16 : 32 * p + 17], (8, LANES)),
        )
        for p in range(2)
    ]
    lane = lax.broadcasted_iota(jnp.int32, (HALF, LANES), 1)
    values = dot_halves((fourth[0], fourth[1]), halves(jnp.concatenate(columns, axis=1)))
    for p in range(2):
        for x in range(PLANES):
            re = values[x * HALF : (x + 1) * HALF, p * LANES : (p + 1) * LANES]
            im = values[ROWS + x * HALF : ROWS + (x + 1) * HALF, p * LANES : (p + 1) * LANES]
            even = jnp.where(lane < NZ, re, pltpu.roll(im, NZ, 1))
            odd = jnp.where(lane < NZ, pltpu.roll(re, NZ, 1), im)
            potential[p, x, pl.ds(0, HALF, stride=2), :] = even + shift[p][x : x + 1]
            potential[p, x, pl.ds(1, HALF, stride=2), :] = odd + shift[p][x : x + 1]
    lane = lax.broadcasted_iota(jnp.int32, (1, LANES), 1)
    same = total(level * plane) * (1.0 / 16)
    cross = total(level * pltpu.roll(plane, 96, 1)) * (1.0 / 16)
    swapped = total(jnp.where(lane < 16, -level * pltpu.roll(plane, 80, 1), level * pltpu.roll(plane, 112, 1))) * (1.0 / 16)
    ahead = lane < 32
    extra = [jnp.where(ahead, same, 0.0), jnp.where(ahead, 0.0, same), jnp.where(ahead, cross, 0.0), jnp.where(ahead, swapped, 0.0)]
    sums = ends[0:PLANES]
    for s in range(1, PARTS):
        sums += ends[s * PLANES : (s + 1) * PLANES]
    sums = jnp.where(lane < LANES // 2, 0.0, sums) + jnp.concatenate(extra, axis=0)
    sums = jnp.sum(sums, axis=1, keepdims=True) * (1.0 / CELLS)
    c00, c11, re, im = (sums[k : k + 1] for k in range(4))
    row = lax.broadcasted_iota(jnp.int32, (2, 2), 0)
    col = lax.broadcasted_iota(jnp.int32, (2, 2), 1)
    coulomb[0] = jnp.where(row == col, jnp.where(row == 0, c00, c11), re)
    coulomb[1] = jnp.where(row == col, 0.0, jnp.where(row == 0, im, -im))


def full(memory_space=pltpu.VMEM):
    return pl.BlockSpec(memory_space=memory_space)


def call(kernel, name, out_shape, *operands, scalars=0, space=pltpu.VMEM, scratch=(), limit=32):
    specs = [full(pltpu.SMEM)] * scalars + [full(space)] * (len(operands) - scalars)
    several = isinstance(out_shape, (list, tuple))
    return pl.pallas_call(
        kernel,
        out_shape=out_shape,
        in_specs=specs,
        out_specs=[full()] * len(out_shape) if several else full(),
        scratch_shapes=scratch,
        compiler_params=pltpu.CompilerParams(vmem_limit_bytes=limit * 1024 * 1024),
        name=name,
    )(*operands)


def shape(*dims, dtype=jnp.float32):
    return jax.ShapeDtypeStruct(dims, dtype)


def tiled_states(states):
    bands = states.shape[1]
    parts = states.reshape(bands, 2, PLANES, HALF, LANES)
    return parts.transpose(0, 1, 3, 2, 4).reshape(bands, 2, ROWS, LANES)


def split_table(values):
    top = values.astype(ml_dtypes.bfloat16)
    rest = (values - top.astype(np.float32)).astype(ml_dtypes.bfloat16)
    return jnp.asarray(np.stack([top, rest]))


def shards(electrons, holes, pair_order):
    found = tables()
    t = {name: jnp.asarray(value) for name, value in found.items()}
    for name in ("first", "second", "third", "fourth"):
        t[name] = split_table(found[name])
    groups = lax.axis_size("blk")
    rank = lax.axis_index("space").astype(jnp.int32).reshape(1)
    previous = lax.ppermute(holes, "blk", [((i - 1) % groups, i) for i in range(groups)])
    e = tiled_states(electrons)
    spectra = shape(ROWS, 2 * LANES)
    h = tiled_states(holes)
    brought = (e, h, t["first"], t["second"], t["twiddle"], t["decay"])
    pack = call(
        own_kernel, "own_pair", shape(PACKED, LANES), rank, pair_order, *brought, t["parts"], t["uniform"],
        scalars=2, space=pltpu.HBM, limit=60,
        scratch=[pltpu.VMEM(x.shape, x.dtype) for x in brought] + [pltpu.SemaphoreType.DMA((8,))],
    )
    pack = call(hold_kernel, "hold", shape(PACKED, LANES), pack)
    far, sent = call(
        far_kernel, "far_pair", [spectra, shape(PARTS * 16, LANES)],
        pack, e, tiled_states(previous), t["first"], t["twiddle"], t["second"], t["decay"],
    )
    blocks = lax.all_to_all(sent.reshape(PARTS, 16, LANES), "space", split_axis=0, concat_axis=0, tiled=True)
    effects, local = call(
        screen_kernel, "screen", [shape(PARTS * STRIDE, LANES), shape(2, ROWS, 2 * LANES)],
        blocks, pack, far, t["green"], t["decay"],
    )
    effects = effects.reshape(PARTS, STRIDE // 4, 4, LANES)
    effects = lax.all_to_all(effects, "space", split_axis=0, concat_axis=0, tiled=True)
    potential, coulomb = call(
        field_kernel, "field", [shape(2, PLANES, NY, LANES), shape(2, 2, 2)],
        effects.reshape(PARTS * STRIDE, LANES), local, t["decay"], t["twiddle"], t["third"], t["fourth"], t["uniform"], pack,
    )
    return (potential[None], coulomb[None])


def solution(mesh):
    in_specs = (
        P("blk", None, None, "space", None),
        P("blk", None, None, "space", None),
        P("blk", None),
    )
    out_specs = (P("blk", None, "space", None, None), P("blk", None, None, None))
    return jax.shard_map(shards, mesh=mesh, in_specs=in_specs, out_specs=out_specs, check_vma=False)
```

```python
import math

import jax
import jax.numpy as jnp
import ml_dtypes
import numpy as np
from jax import lax
from jax.experimental import pallas as pl
from jax.experimental.pallas import tpu as pltpu
from jax.sharding import PartitionSpec as P

NX = 64
NY = 64
NZ = 64
CELLS = NX * NY * NZ
SCREENING = 0.01
PARTS = 16
PLANES = NX // PARTS
HALF = NY // 2
ROWS = HALF * PLANES
LANES = 128
SUMS, PART, LINE, MASK, LOCAL, TERM, PACKED = 256, 384, 408, 416, 424, 680, 688
STRIDE = 20


def turn(angles, sign):
    cosines, sines = np.cos(angles), sign * np.sin(angles)
    return np.array([[cosines, -sines], [sines, cosines]])


def tables():
    half, full = np.arange(HALF), np.arange(NY)
    two = np.arange(2)
    eye_x = np.eye(PLANES)
    order = np.array([2 * d + kl for kl in range(2) for d in range(PARTS)])
    rows = turn(2 * math.pi * (np.outer(order, half) % HALF) / HALF, -1)
    first = np.einsum("dckn,yx->dykcnx", rows, eye_x).reshape(2 * ROWS, 2 * ROWS)
    angles = 2 * math.pi / NY * order[None, :, None, None] * two[None, None, :, None]
    angles = np.broadcast_to(angles, (PLANES, HALF, 2, NZ)).reshape(ROWS, LANES)
    twiddle = np.stack([np.cos(angles), np.sin(angles)])
    depth = turn(2 * math.pi * (np.outer(full, full) % NZ) / NZ, -1)
    signs = np.array([[1.0, 1.0], [1.0, -1.0]])
    second = np.einsum("dckz,hb->cbzdhk", depth, signs).reshape(2 * LANES, 2 * LANES)
    term = 2.0 - 2.0 * np.cos(2 * math.pi * full / 64)
    excess = term[:, None] + term[None, :] + SCREENING
    kappa = 2.0 * np.arcsinh(0.5 * np.sqrt(excess))
    kappa = kappa.reshape(2, HALF, NZ).transpose(1, 0, 2).reshape(HALF, LANES)
    green = 1.0 / (2.0 * np.sinh(kappa)) / (NY * NZ)
    green[0, 0] = 0.0
    decay = np.stack([np.exp(-kappa * n)[order] for n in (1, 2, 3)])
    step = np.exp(-PLANES * kappa)
    close = 1.0 / (1.0 - np.exp(-NX * kappa))
    near = green * np.exp(-kappa)
    parts = np.stack([step, close, near]).reshape(3, PARTS, 1, 2, LANES)
    parts = np.broadcast_to(parts, (3, PARTS, 4, 2, LANES)).transpose(1, 0, 2, 3, 4).reshape(PARTS, 24, LANES)
    line = np.array([0.0] + [1.0 / (t + SCREENING) for t in term[1:]])
    along = np.cos(2 * math.pi * (np.outer(full, full) % NX) / NX) @ line / NX / (NY * NZ)
    lag = along[(full[:, None] - full[None, :]) % NX]
    uniform = np.zeros((PARTS, 8, LANES))
    uniform[:, :PLANES, :NX] = lag.reshape(PARTS, PLANES, NX)
    back = turn(2 * math.pi * (np.outer(full, full) % NZ) / NZ, 1)
    third = np.einsum("dczk,hb->chkdbz", back, signs).reshape(2 * LANES, 2 * LANES)
    columns = turn(2 * math.pi * (np.outer(half, order) % HALF) / HALF, 1)
    fourth = np.einsum("dcnk,yx->dyncxk", columns, eye_x).reshape(2 * ROWS, 2 * ROWS)
    names = ("first", "twiddle", "second", "green", "decay", "parts", "uniform", "third", "fourth")
    values = (first, twiddle, second, green[order], decay, parts, uniform, third, fourth)
    return {n: np.ascontiguousarray(v, dtype=np.float32) for n, v in zip(names, values)}


def dot(a, b):
    return jnp.dot(a, b, precision=lax.Precision.HIGHEST, preferred_element_type=jnp.float32)


def halves(values):
    top = values.astype(jnp.bfloat16)
    return top, (values - top.astype(jnp.float32)).astype(jnp.bfloat16)


def dot_halves(a, b):
    def product(x, y):
        return jnp.dot(x, y, preferred_element_type=jnp.float32)

    return product(a[0], b[0]) + (product(a[0], b[1]) + product(a[1], b[0]))


def left_halves(table, values):
    parts = halves(values)
    width = values.shape[1]
    both = jnp.dot(table[0], jnp.concatenate(parts, axis=1), preferred_element_type=jnp.float32)
    rest = jnp.dot(table[1], parts[0], preferred_element_type=jnp.float32)
    return both[:, :width] + (both[:, width:] + rest)


def right_halves(values, table):
    parts = halves(values)
    height = values.shape[0]
    both = jnp.dot(jnp.concatenate(parts, axis=0), table[0], preferred_element_type=jnp.float32)
    rest = jnp.dot(parts[0], table[1], preferred_element_type=jnp.float32)
    return both[:height] + (both[height:] + rest)


def with_first_row(values, rows):
    first = lax.broadcasted_iota(jnp.int32, (8, values.shape[1]), 0) == 0
    pieces = []
    for x in range(PLANES):
        own = values[x * HALF : (x + 1) * HALF]
        pieces += [jnp.where(first, rows[x : x + 1], own[:8]), own[8:]]
    return jnp.concatenate(pieces, axis=0)


def density_spectra(electrons, holes, first, twiddle, second):
    real = jnp.zeros((ROWS, LANES), jnp.float32)
    imag = jnp.zeros((ROWS, LANES), jnp.float32)
    for band in range(electrons.shape[0]):
        e_re = electrons[band, 0].astype(jnp.float32)
        e_im = electrons[band, 1].astype(jnp.float32)
        h_re = holes[band, 0].astype(jnp.float32)
        h_im = holes[band, 1].astype(jnp.float32)
        real += e_re * h_re + e_im * h_im
        imag += e_re * h_im - e_im * h_re
    around, column, level = [], [], []
    for part in (real, imag):
        rows = part[0:8]
        for k in range(1, ROWS // 8):
            rows = rows + part[k * 8 : k * 8 + 8]
        mean = (rows[0:4] + rows[4:8]) * (1.0 / HALF)
        grand = jnp.sum(mean, axis=1, keepdims=True) * (1.0 / LANES)
        around.append(part - jnp.concatenate([mean] * HALF, axis=0))
        column.append((mean - grand) * HALF)
        level.append(grand * (NY * NZ))
    mixed = left_halves(first, jnp.concatenate(around, axis=0))
    u_re, u_im = mixed[:ROWS], mixed[ROWS:]
    t_re = with_first_row(u_re * twiddle[0] + u_im * twiddle[1], column[0])
    t_im = with_first_row(u_im * twiddle[0] - u_re * twiddle[1], column[1])
    values = right_halves(jnp.concatenate([t_re, t_im], axis=1), second)
    lane = lax.broadcasted_iota(jnp.int32, (PLANES, LANES), 1)
    parts = []
    for c in range(2):
        part = values[:, c * LANES : (c + 1) * LANES]
        rows = jnp.concatenate([part[x * HALF : x * HALF + 1] for x in range(PLANES)], axis=0)
        parts.append(with_first_row(part, rows + jnp.where(lane == 0, level[c], 0.0)))
    return jnp.concatenate(parts, axis=1)


def planes_of(spectra, c):
    return [spectra[x * HALF : (x + 1) * HALF, c * LANES : (c + 1) * LANES] for x in range(PLANES)]


def moments(spectra, decay):
    found = [[None, None], [None, None]]
    for c in range(2):
        planes = planes_of(spectra, c)
        for way, run in enumerate((planes, planes[::-1])):
            total = run[0]
            for plane in run[1:]:
                total = total * decay + plane
            found[way][c] = total
    return found


def total(values):
    return jnp.sum(values, axis=0, keepdims=True)


def local_fields(values, green, decay):
    weight = [green[...]] + [green[...] * decay[n] for n in range(3)]
    density, field = {}, {}
    for c in range(2):
        planes = planes_of(values, c)
        for x in range(PLANES):
            value = weight[0] * planes[x]
            for other in range(PLANES):
                if other != x:
                    value += weight[abs(x - other)] * planes[other]
            density[c, x], field[c, x] = planes[x], value
    return density, field


def same_term(density, field):
    return total(sum(field[key] * density[key] for key in field))


def own_kernel(rank, order, *refs):
    sources, pack, copies, sems = refs[:9], refs[9], refs[10:17], refs[17]
    me = rank[0]
    sources = sources[:7] + (sources[7].at[me], sources[8].at[me])
    targets = copies + (pack.at[PART : PART + 24], pack.at[LINE : LINE + 8])
    moves = [
        pltpu.make_async_copy(source, target, sems.at[n])
        for n, (source, target) in enumerate(zip(sources, targets))
    ]
    for move in moves:
        move.start()
    pack[MASK : MASK + 8] = jnp.full((8, LANES), order[0, 0], jnp.int32).astype(jnp.float32)
    for move in moves:
        move.wait()
    electrons, holes, first, second, twiddle, decay, green = copies
    values = density_spectra(electrons, holes, first, twiddle, second)
    found = moments(values, decay[0])
    for c in range(2):
        pack[c * ROWS : (c + 1) * ROWS] = values[:, c * LANES : (c + 1) * LANES]
        for way in range(2):
            row = SUMS + (way * 2 + c) * HALF
            pack[row : row + HALF] = found[way][c]
    density, field = local_fields(values, green, decay)
    for c in range(2):
        for x in range(PLANES):
            row = LOCAL + c * ROWS + x * HALF
            pack[row : row + HALF] = field[c, x]
    pack[TERM : TERM + 8] = jnp.broadcast_to(same_term(density, field), (8, LANES))


def hold_kernel(source, target):
    target[...] = source[...]


def far_kernel(pack, electrons, holes, first, twiddle, second, decay, spectra, out):
    values = density_spectra(electrons, holes, first, twiddle, second)
    spectra[...] = values
    found = moments(values, decay[0])
    for way in range(2):
        for c in range(2):
            row = SUMS + (way * 2 + c) * HALF
            pair = (pack[row : row + HALF], found[way][c])
            for p in range(2):
                for kl in range(2):
                    row = way * 8 + p * 4 + c * 2 + kl
                    out[pl.ds(row, PARTS, stride=16), :] = pair[p][kl * PARTS : (kl + 1) * PARTS]


def local_terms(pack, far, green, decay, local):
    far_density, far_field = local_fields(far[...], green, decay)
    density, field = {}, {}
    for c in range(2):
        for x in range(PLANES):
            row = c * ROWS + x * HALF
            density[0, c, x], field[0, c, x] = pack[row : row + HALF], pack[LOCAL + row : LOCAL + row + HALF]
            density[1, c, x] = far_density[c, x]
            local[x * HALF : (x + 1) * HALF, c * LANES : (c + 1) * LANES] = far_field[c, x]
    cross = jnp.zeros((HALF, LANES), jnp.float32)
    swapped = jnp.zeros((HALF, LANES), jnp.float32)
    for x in range(PLANES):
        for c in range(2):
            cross += field[0, c, x] * density[1, c, x]
        swapped += field[0, 1, x] * density[1, 0, x] - field[0, 0, x] * density[1, 1, x]
    terms = [pack[TERM : TERM + 1], same_term(far_density, far_field), total(cross), total(swapped)]
    lane = lax.broadcasted_iota(jnp.int32, (1, LANES), 1)
    rows = []
    for x in range(PLANES):
        row = jnp.zeros((1, LANES), jnp.float32)
        for p in range(2):
            for c in range(2):
                value = jnp.broadcast_to(density[p, c, x][0:1, 0:1], (1, LANES))
                row = jnp.where(lane // 16 == p * 2 + c, value, row)
        rows.append(row)
    return jnp.concatenate(rows, axis=0), terms


def screen_kernel(block, pack, far, green, decay, out, local):
    ends, inner = local_terms(pack, far, green, decay, local)
    step, close, near = (pack[PART + 8 * n : PART + 8 * n + 8] for n in range(3))
    right = [block[s, 0:8] for s in range(PARTS)]
    left = [block[s, 8:16] for s in range(PARTS)]
    from_right, from_left = right[0], left[PARTS - 1]
    for n in range(1, PARTS):
        from_right = from_right * step + right[n]
        from_left = from_left * step + left[PARTS - 1 - n]
    from_right, from_left = from_right * close, from_left * close
    effect = {}
    for n in range(PARTS):
        effect[0, n] = near * from_right
        effect[1, PARTS - 1 - n] = near * from_left
        from_right = from_right * step + right[n]
        from_left = from_left * step + left[PARTS - 1 - n]
    zero = jnp.zeros((8, LANES), jnp.float32)
    same, cross, swapped = zero, zero, zero
    for s in range(PARTS):
        for way, moment in ((0, left[s]), (1, right[s])):
            value = effect[way, s]
            out[s * STRIDE + way * 8 : s * STRIDE + way * 8 + 8] = value
            turned = jnp.concatenate([moment[4:8], moment[0:4]], axis=0)
            same += value * moment
            cross += value * turned
            swapped += value * jnp.concatenate([moment[6:8], moment[4:6], moment[0:4]], axis=0)
    terms = [
        total(same[0:4]),
        total(same[4:8]),
        total(cross[0:4]),
        total(swapped[2:4]) - total(swapped[0:2]),
    ]
    terms = jnp.concatenate([a + b for a, b in zip(inner, terms)], axis=0)
    terms += pltpu.roll(terms, LANES // 2, 1)
    lane = lax.broadcasted_iota(jnp.int32, (PLANES, LANES), 1)
    ends = jnp.where(lane < LANES // 2, ends, terms)
    for s in range(PARTS):
        out[s * STRIDE + 16 : s * STRIDE + 20] = ends


def field_kernel(block, local, decay, twiddle, third, fourth, uniform, pack, potential, coulomb):
    weight = [None, decay[0], decay[1], decay[2]]
    first = jnp.clip(jnp.max(pack[MASK : MASK + 1, 0:1]).astype(jnp.int32), 0, 1)

    def effect(way, p, c):
        rows = [block[pl.ds(way * 8 + p * 4 + c * 2 + kl, PARTS, stride=STRIDE), :] for kl in range(2)]
        return jnp.concatenate(rows, axis=0)

    pairs = []
    for p in range(2):
        parts = []
        for c in range(2):
            right, left = effect(0, p, c), effect(1, p, c)
            planes = []
            for x in range(PLANES):
                if p == 0:
                    row = LOCAL + c * ROWS + x * HALF
                    value = pack[row : row + HALF]
                else:
                    value = local[x * HALF : (x + 1) * HALF, c * LANES : (c + 1) * LANES]
                value += right if x == 0 else right * weight[x]
                value += left if x == PLANES - 1 else left * weight[PLANES - 1 - x]
                planes.append(value)
            parts.append(jnp.concatenate(planes, axis=0))
        pairs.append(jnp.concatenate(parts, axis=1))
    mixed = dot_halves(halves(jnp.concatenate(pairs, axis=0)), (third[0], third[1]))
    columns = []
    for p in range(2):
        u_re, u_im = mixed[p * ROWS : (p + 1) * ROWS, :LANES], mixed[p * ROWS : (p + 1) * ROWS, LANES:]
        t_re = u_re * twiddle[0] - u_im * twiddle[1]
        t_im = u_im * twiddle[0] + u_re * twiddle[1]
        columns.append(jnp.concatenate([t_re, t_im], axis=0))
    ends = jnp.concatenate([block[STRIDE * s + 16 : STRIDE * s + 20] for s in range(PARTS)], axis=0)
    lane = lax.broadcasted_iota(jnp.int32, (NX, LANES), 1)
    plane = jnp.where(lane < LANES // 2, ends, 0.0)
    plane = plane - total(plane) * (1.0 / NX)
    lags = [uniform[s, 0:PLANES, 0:NX] for s in range(PARTS)] + [pack[LINE : LINE + 8, 0:NX]]
    level = dot(jnp.concatenate(lags, axis=0), plane)
    level, own = level[:NX], level[NX:]
    lane = lax.broadcasted_iota(jnp.int32, (8, LANES), 1)
    shift = [
        jnp.where(
            lane < NZ,
            jnp.broadcast_to(own[:, 32 * p : 32 * p + 1], (8, LANES)),
            jnp.broadcast_to(own[:, 32 * p + 16 : 32 * p + 17], (8, LANES)),
        )
        for p in range(2)
    ]
    lane = lax.broadcasted_iota(jnp.int32, (HALF, LANES), 1)
    values = dot_halves((fourth[0], fourth[1]), halves(jnp.concatenate(columns, axis=1)))
    for p in range(2):
        place = first if p == 0 else 1 - first
        for x in range(PLANES):
            re = values[x * HALF : (x + 1) * HALF, p * LANES : (p + 1) * LANES]
            im = values[ROWS + x * HALF : ROWS + (x + 1) * HALF, p * LANES : (p + 1) * LANES]
            even = jnp.where(lane < NZ, re, pltpu.roll(im, NZ, 1))
            odd = jnp.where(lane < NZ, pltpu.roll(re, NZ, 1), im)
            potential[place, x, pl.ds(0, HALF, stride=2), :] = even + shift[p][x : x + 1]
            potential[place, x, pl.ds(1, HALF, stride=2), :] = odd + shift[p][x : x + 1]
    lane = lax.broadcasted_iota(jnp.int32, (1, LANES), 1)
    same = total(level * plane) * (1.0 / 16)
    cross = total(level * pltpu.roll(plane, 96, 1)) * (1.0 / 16)
    swapped = total(jnp.where(lane < 16, -level * pltpu.roll(plane, 80, 1), level * pltpu.roll(plane, 112, 1))) * (1.0 / 16)
    ahead = lane < 32
    extra = [jnp.where(ahead, same, 0.0), jnp.where(ahead, 0.0, same), jnp.where(ahead, cross, 0.0), jnp.where(ahead, swapped, 0.0)]
    sums = ends[0:PLANES]
    for s in range(1, PARTS):
        sums += ends[s * PLANES : (s + 1) * PLANES]
    sums = jnp.where(lane < LANES // 2, 0.0, sums) + jnp.concatenate(extra, axis=0)
    sums = jnp.sum(sums, axis=1, keepdims=True) * (1.0 / CELLS)
    own, far, re, im = (sums[k : k + 1] for k in range(4))
    straight = pack[MASK : MASK + 1, 0:1] < 0.5
    c00, c11, im = jnp.where(straight, own, far), jnp.where(straight, far, own), jnp.where(straight, im, -im)
    row = lax.broadcasted_iota(jnp.int32, (2, 2), 0)
    col = lax.broadcasted_iota(jnp.int32, (2, 2), 1)
    coulomb[0] = jnp.where(row == col, jnp.where(row == 0, c00, c11), re)
    coulomb[1] = jnp.where(row == col, 0.0, jnp.where(row == 0, im, -im))


def full(memory_space=pltpu.VMEM):
    return pl.BlockSpec(memory_space=memory_space)


def call(kernel, name, out_shape, *operands, scalars=0, space=pltpu.VMEM, scratch=(), limit=32):
    specs = [full(pltpu.SMEM)] * scalars + [full(space)] * (len(operands) - scalars)
    several = isinstance(out_shape, (list, tuple))
    return pl.pallas_call(
        kernel,
        out_shape=out_shape,
        in_specs=specs,
        out_specs=[full()] * len(out_shape) if several else full(),
        scratch_shapes=scratch,
        compiler_params=pltpu.CompilerParams(vmem_limit_bytes=limit * 1024 * 1024),
        name=name,
    )(*operands)


def shape(*dims, dtype=jnp.float32):
    return jax.ShapeDtypeStruct(dims, dtype)


def tiled_states(states):
    bands = states.shape[1]
    parts = states.reshape(bands, 2, PLANES, HALF, LANES)
    return parts.transpose(0, 1, 3, 2, 4).reshape(bands, 2, ROWS, LANES)


def split_table(values):
    top = values.astype(ml_dtypes.bfloat16)
    rest = (values - top.astype(np.float32)).astype(ml_dtypes.bfloat16)
    return jnp.asarray(np.stack([top, rest]))


def shards(electrons, holes, pair_order):
    found = tables()
    t = {name: jnp.asarray(value) for name, value in found.items()}
    for name in ("first", "second", "third", "fourth"):
        t[name] = split_table(found[name])
    groups = lax.axis_size("blk")
    rank = lax.axis_index("space").astype(jnp.int32).reshape(1)
    previous = lax.ppermute(holes, "blk", [((i - 1) % groups, i) for i in range(groups)])
    e = tiled_states(electrons)
    spectra = shape(ROWS, 2 * LANES)
    h = tiled_states(holes)
    brought = (e, h, t["first"], t["second"], t["twiddle"], t["decay"], t["green"])
    pack = call(
        own_kernel, "own_pair", shape(PACKED, LANES), rank, pair_order, *brought, t["parts"], t["uniform"],
        scalars=2, space=pltpu.HBM, limit=60,
        scratch=[pltpu.VMEM(x.shape, x.dtype) for x in brought] + [pltpu.SemaphoreType.DMA((9,))],
    )
    pack = call(hold_kernel, "hold", shape(PACKED, LANES), pack)
    far, sent = call(
        far_kernel, "far_pair", [spectra, shape(PARTS * 16, LANES)],
        pack, e, tiled_states(previous), t["first"], t["twiddle"], t["second"], t["decay"],
    )
    blocks = lax.all_to_all(sent.reshape(PARTS, 16, LANES), "space", split_axis=0, concat_axis=0, tiled=True)
    effects, local = call(
        screen_kernel, "screen", [shape(PARTS * STRIDE, LANES), shape(ROWS, 2 * LANES)],
        blocks, pack, far, t["green"], t["decay"],
    )
    effects = effects.reshape(PARTS, STRIDE // 4, 4, LANES)
    effects = lax.all_to_all(effects, "space", split_axis=0, concat_axis=0, tiled=True)
    potential, coulomb = call(
        field_kernel, "field", [shape(2, PLANES, NY, LANES), shape(2, 2, 2)],
        effects.reshape(PARTS * STRIDE, LANES), local, t["decay"], t["twiddle"], t["third"], t["fourth"], t["uniform"], pack,
    )
    return (potential[None], coulomb[None])


def solution(mesh):
    in_specs = (
        P("blk", None, None, "space", None),
        P("blk", None, None, "space", None),
        P("blk", None),
    )
    out_specs = (P("blk", None, "space", None, None), P("blk", None, None, None))
    return jax.shard_map(shards, mesh=mesh, in_specs=in_specs, out_specs=out_specs, check_vma=False)
```
